256 devices in a mesh: row: 16 (over y, z_hi, core), col: 16 (over z_lo, x).
Axes of the slice: x: 4, y: 4, z: 8 (z_hi: 2, z_lo: 4; z = z_hi * 4 + z_lo), core: 2. Of those that a mesh axis runs over, the one named last changes fastest.
Arguments:
- object_field: float32 [2, 4096, 4096], P(None, 'row', 'col')
- probe_field: float32 [2, 128, 128], replicated, may hold values from -6 to 6
- amplitudes: float32 [2, 16, 16, 16, 128, 128], P(None, 'row', 'col'), may hold values from 0 to 2
- positions: int32 [2, 2, 16, 16, 16], P(None, None, 'row', 'col'), may hold values from 8 to 4087, as said below
- shifts: int32 [2, 2, 16, 16, 16], P(None, None, 'row', 'col'), may hold values from -8 to 8
Outputs:
- new_object: float32 [2, 4096, 4096], P(None, 'row', 'col')
- new_probe: float32 [2, 128, 128], replicated
The draws below stay inside these ranges and needn't reach their ends.
Inputs may be any that keep to these rules, and one draw needn't show every extreme that they name: For a pattern stored at tile (r, c), positions plus shifts lie in r * 256 .. r * 256 + 255 for the first coordinate and c * 256 .. c * 256 + 255 for the second.
All inputs are finite; a program needn't handle non-finite values.
Results may differ from the reference program's by a relative error of at most 0.0003.
Values sent between devices are 32-bit elements; how exact they have to be, the bound alone decides.
A program may use at most 64 MiB of HBM per device.

```python
import math
import jax
import jax.numpy as jnp
from jax import lax

PROBE = 128
TILE = 256
B = 16
ITERS = 2
SHIFT_MAX = 8
NXG = 4096
NYG = 4096
PATTERNS = 4096
N_ROW = 16
N_COL = 16


def draw_object_field(key, part):
    key = jax.random.fold_in(key, 5)
    key_size, key_phase = jax.random.split(key)
    profile = 1.0 + 2.0 * jnp.arange(NXG, dtype=jnp.float32)[:, None] / NXG
    magnitude = jax.random.uniform(key_size, (NXG, NYG), jnp.float32, 0.5, 1.5)
    phase = jax.random.uniform(key_phase, (NXG, NYG), jnp.float32, -math.pi, math.pi)
    amount = magnitude * profile
    return jnp.stack([amount * jnp.cos(phase), amount * jnp.sin(phase)]).astype(jnp.float32)


def draw_positions(key, part):
    key = jax.random.fold_in(key, 9)
    local_cells = jax.random.randint(key, (2, ITERS, N_ROW, N_COL, B), SHIFT_MAX, TILE - SHIFT_MAX, dtype=jnp.int32)
    slot_number = jnp.arange(B, dtype=jnp.int32)[None, None, None, None, :]
    first_round = jnp.arange(ITERS, dtype=jnp.int32)[None, :, None, None, None] == 0
    local_cells = jnp.where(first_round & (slot_number == 0), SHIFT_MAX, local_cells)
    local_cells = jnp.where(first_round & (slot_number == 1), TILE - SHIFT_MAX - 1, local_cells)
    row_offset = jnp.broadcast_to((jnp.arange(N_ROW, dtype=jnp.int32) * TILE)[None, None, :, None, None], (1, ITERS, N_ROW, N_COL, B))
    col_offset = jnp.broadcast_to((jnp.arange(N_COL, dtype=jnp.int32) * TILE)[None, None, None, :, None], (1, ITERS, N_ROW, N_COL, B))
    offsets = jnp.concatenate([row_offset, col_offset], axis=0)
    return (local_cells + offsets).astype(jnp.int32)


def with_ends(array, stream_key, smallest, high):
    spot = [jax.random.randint(jax.random.fold_in(stream_key, axis), (), 0, length) for axis, length in enumerate(array.shape)]
    longest = array.shape.index(max(array.shape))
    next_to = spot[:longest] + [(spot[longest] + 1) % array.shape[longest]] + spot[longest + 1:]
    return array.at[tuple(spot)].set(smallest).at[tuple(next_to)].set(high)


def shard_levels(key, shape, shards, least, largest):
    loudness, own = 1.0, jax.random.fold_in(key, 6)
    for position, shards_of in shards:
        draws = jnp.exp(jax.random.uniform(jax.random.fold_in(own, position), (shards_of,), jnp.float32, least / len(shards), largest / len(shards)))
        loudness = loudness * jnp.repeat(draws, shape[position] // shards_of).reshape([-1 if axis == position else 1 for axis in range(len(shape))])
    return loudness


def noise(rng, dims, scale, reach, held_as=jnp.bfloat16):
    entries = jax.random.normal(rng, dims, jnp.float32) * scale
    return jnp.minimum(jnp.maximum(entries, -reach), reach).astype(held_as)


def setup_inputs(seed: int = 0) -> dict:
    key_of = jax.random.split(jax.random.key(seed), 6)
    object_field = draw_object_field(jax.random.fold_in(key_of[5], 71), 0)
    probe_field = noise(key_of[1], (2, PROBE, PROBE), 1.0, 6.0, jnp.float32)
    amplitudes = jnp.clip(2.0 * jax.random.uniform(key_of[2], (ITERS, N_ROW, N_COL, B, PROBE, PROBE), jnp.float32) ** shard_levels(key_of[2], (ITERS, N_ROW, N_COL, B, PROBE, PROBE), ((1, 16), (2, 16)), -0.2, 0.2), 0.0, 2.0)
    positions = draw_positions(jax.random.fold_in(key_of[5], 71), 0)
    shifts = with_ends(jax.random.randint(key_of[4], (2, ITERS, N_ROW, N_COL, B), 0 - SHIFT_MAX, SHIFT_MAX + 1), jax.random.fold_in(key_of[4], 1), 0 - SHIFT_MAX, SHIFT_MAX).astype(jnp.int32)
    return {"object_field": object_field, "probe_field": probe_field, "amplitudes": amplitudes, "positions": positions, "shifts": shifts}


def cut_patch(padded, row_start, col_start):
    first_axis = jnp.zeros((), jnp.int32)
    return lax.dynamic_slice(padded, (first_axis, row_start.astype(jnp.int32), col_start.astype(jnp.int32)), (2, PROBE, PROBE))

def reference(object_field, probe_field, amplitudes, positions, shifts):
    half = PROBE // 2
    probe_re = probe_field[0]
    probe_im = probe_field[1]
    for iteration in range(ITERS):
        padded = jnp.pad(object_field, ((0, 0), (half, half), (half, half)))
        rows_at = (positions[0, iteration] + shifts[0, iteration]).reshape(-1, B).astype(jnp.int32)
        cols_at = (positions[1, iteration] + shifts[1, iteration]).reshape(-1, B).astype(jnp.int32)
        measured = amplitudes[iteration].reshape(-1, B, PROBE, PROBE)

        def block_step(carry, inputs):
            grad_total, terms = carry
            block_rows, block_cols, block_amp = inputs
            patches = jax.vmap(cut_patch, in_axes=(None, 0, 0))(padded, block_rows, block_cols)
            obj_re = patches[:, 0]
            obj_im = patches[:, 1]
            exit_re = probe_re * obj_re - probe_im * obj_im
            exit_im = probe_re * obj_im + probe_im * obj_re
            spectrum = jnp.fft.fft2(exit_re + 1j * exit_im, norm='ortho')
            four_re = jnp.real(spectrum)
            four_im = jnp.imag(spectrum)
            magnitude = jnp.sqrt(four_re * four_re + four_im * four_im)
            keep = 1.0 - block_amp / jnp.maximum(magnitude, 1.0)
            inverse = jnp.fft.ifft2(keep * four_re + 1j * (keep * four_im), norm='ortho')
            back_re = jnp.real(inverse)
            back_im = jnp.imag(inverse)
            grad_re = probe_re * back_re + probe_im * back_im
            grad_im = probe_re * back_im - probe_im * back_re
            q_real = lax.optimization_barrier(jnp.sum(obj_re * back_re + obj_im * back_im, axis=0))
            q_imag = lax.optimization_barrier(jnp.sum(obj_re * back_im - obj_im * back_re, axis=0))
            weight = lax.optimization_barrier(jnp.sum(obj_re * obj_re + obj_im * obj_im, axis=0))
            terms = terms + jnp.stack([q_real, q_imag, weight])

            def add_patch(number, total):
                first_axis = jnp.zeros((), jnp.int32)
                start = (first_axis, block_rows[number].astype(jnp.int32), block_cols[number].astype(jnp.int32))
                piece = jnp.stack([grad_re[number], grad_im[number]])
                current = lax.dynamic_slice(total, start, (2, PROBE, PROBE))
                return lax.dynamic_update_slice(total, current + piece, start)
            grad_total = lax.fori_loop(0, B, add_patch, grad_total)
            return ((grad_total, terms), None)
        start_grad = jnp.zeros(padded.shape, jnp.float32)
        start_terms = jnp.zeros((3, PROBE, PROBE), jnp.float32)
        (grad_total, terms), unused = lax.scan(block_step, (start_grad, start_terms), (rows_at, cols_at, measured))
        gradient = grad_total[:, half:half + NXG, half:half + NYG]
        step = 0.5 / (jnp.max(probe_re * probe_re + probe_im * probe_im) + 1e-06)
        object_field = object_field - step * gradient
        denominator = terms[2] + 0.2 * PATTERNS
        probe_re = probe_re - terms[0] / denominator
        probe_im = probe_im - terms[1] / denominator
    return (object_field, jnp.stack([probe_re, probe_im]))
```

```python
import functools
import math

import jax
import jax.numpy as jnp
import ml_dtypes
import numpy as np
from jax import lax
from jax.experimental import pallas as pl
from jax.experimental.pallas import tpu as pltpu
from jax.sharding import PartitionSpec as P

MESH = pl.DeviceIdType.MESH
F32 = jnp.float32
BF16 = jnp.bfloat16

WIDTH = 128
HALF = 64
TILE = 256
PAD = TILE + 2 * HALF
BLOCKS = 4
BATCH = 16
ITERS = 2
N_ROW = 16
N_COL = 16
NX, NY, NZ = 4, 4, 8
PATTERNS = BATCH * N_ROW * N_COL
TERM_ROWS = 3 * WIDTH
CORE_ROWS = TERM_ROWS // 2
CHUNK = CORE_ROWS // NZ
CENTRE = 256
PLACED = CENTRE + WIDTH + 256


def tables():
    n = np.arange(WIDTH)
    angle = (np.outer(n, n) % WIDTH) * (2.0 * math.pi / WIDTH)
    c, s = np.cos(angle) / math.sqrt(WIDTH), np.sin(angle) / math.sqrt(WIDTH)
    parts = []
    for m in (np.block([[c, s], [-s, c]]), np.block([[c, -s], [s, c]])):
        m = m.astype(np.float32)
        high = m.astype(ml_dtypes.bfloat16)
        parts += [high, (m - high.astype(np.float32)).astype(ml_dtypes.bfloat16)]
    return np.stack(parts)


def split(x):
    high = x.astype(BF16)
    return high, (x - high.astype(F32)).astype(BF16)


def mm(a, b):
    return jnp.dot(a, b, preferred_element_type=F32)


def left_mul(high, low, x):
    xh, xl = split(x)
    return mm(high, xh) + mm(high, xl) + mm(low, xh)


def right_mul(x, high, low):
    xh, xl = split(x)
    return mm(xh, high) + mm(xl, high) + mm(xh, low)


def swap_quadrants(y):
    top = jnp.concatenate([y[:WIDTH, :WIDTH], y[WIDTH:, :WIDTH]], axis=1)
    low = jnp.concatenate([y[:WIDTH, WIDTH:], y[WIDTH:, WIDTH:]], axis=1)
    return jnp.concatenate([top, low], axis=0)


def kernel(
    obj_in, probe_in, amp_in, pos, shf, tab, new_obj, new_probe,
    obj, prb, amp, zb, grad, terms, pack, fold_row, fold_col, fold_cor,
    hpack, hbuf, core_buf, z_buf, xy_buf, total, summed,
    in_sem, halo_s, halo_r, fold_s, fold_r, core_s, core_r, z_s, z_r, xy_s, xy_r,
):
    r, c = lax.axis_index("row"), lax.axis_index("col")
    y, zh, core = r // 4, (r // 2) % 2, r % 2
    zl, x = c // 4, c % 4
    z = zh * 4 + zl
    xy = y * NX + x

    def near(dr, dc):
        return ((r + dr + N_ROW) % N_ROW, (c + dc + N_COL) % N_COL)

    def at_z(d):
        other = (z + d) % NZ
        return (y * 4 + (other // 4) * 2 + core, (other % 4) * 4 + x)

    def at_xy(d):
        other = (xy + d) % (NX * NY)
        return ((other // NX) * 4 + zh * 2 + core, zl * 4 + other % NX)

    partner = (r + 1 - 2 * core, c)
    around = [(-1, 0), (1, 0), (0, -1), (0, 1), (-1, -1), (-1, 1), (1, -1), (1, 1)]

    barrier = pltpu.get_barrier_semaphore()
    peers = [near(*d) for d in around] + [partner]
    peers += [at_z(d) for d in range(1, NZ)] + [at_xy(d) for d in range(1, NX * NY)]
    for peer in peers:
        pl.semaphore_signal(barrier, inc=1, device_id=peer, device_id_type=MESH)

    loads = [
        pltpu.make_async_copy(obj_in.at[:, :, 0:128], obj.at[:, 1, HALF:HALF + TILE], in_sem.at[0]),
        pltpu.make_async_copy(obj_in.at[:, :, 128:256], obj.at[:, 2, HALF:HALF + TILE], in_sem.at[1]),
        pltpu.make_async_copy(probe_in, prb, in_sem.at[2]),
        pltpu.make_async_copy(amp_in.at[:, 0, 0], amp, in_sem.at[3]),
    ]
    for load in loads:
        load.start()

    lane = lax.broadcasted_iota(jnp.int32, (HALF, WIDTH), 1)
    lane_full = lax.broadcasted_iota(jnp.int32, (WIDTH, WIDTH), 1)
    low_half = lane < HALF

    def remote(src, dst, ss, rs, to):
        return pltpu.make_async_remote_copy(
            src_ref=src, dst_ref=dst, send_sem=ss, recv_sem=rs, device_id=to, device_id_type=MESH
        )

    def halo_copies(h):
        src = [
            obj.at[:, 1:3, 64:128], obj.at[:, 1:3, 256:320], hpack.at[h, 0], hpack.at[h, 1],
            hpack.at[h, 0, 0:64], hpack.at[h, 1, 0:64], hpack.at[h, 0, 192:256], hpack.at[h, 1, 192:256],
        ]
        dst = [
            obj.at[:, 1:3, 320:384], obj.at[:, 1:3, 0:64], hbuf.at[h, 0, 64:320], hbuf.at[h, 1, 64:320],
            hbuf.at[h, 0, 320:384], hbuf.at[h, 1, 320:384], hbuf.at[h, 0, 0:64], hbuf.at[h, 1, 0:64],
        ]
        return [
            remote(src[i], dst[i], halo_s.at[h, i], halo_r.at[h, i], near(*around[i])) for i in range(8)
        ]

    def halo_send(h):
        copies = halo_copies(h)
        copies[0].start()
        copies[1].start()
        for t in range(4):
            rows = slice(HALF + 64 * t, HALF + 64 * t + 64)
            to = slice(64 * t, 64 * t + 64)
            hpack[h, 0, to] = jnp.where(low_half, obj[0, 1, rows], pltpu.roll(obj[1, 1, rows], 64, 1))
            hpack[h, 1, to] = jnp.where(low_half, pltpu.roll(obj[0, 2, rows], 64, 1), obj[1, 2, rows])
        for i in (4, 5, 6, 7, 2, 3):
            copies[i].start()
        return copies

    def halo_finish(h, copies):
        for copy in copies:
            copy.wait()
        for t in range(6):
            rows = slice(64 * t, 64 * t + 64)
            inside = r >= 0
            if t == 0:
                inside = r > 0
            if t == 5:
                inside = r < N_ROW - 1
            right = jnp.where(jnp.logical_and(inside, c < N_COL - 1), hbuf[h, 0, rows], 0.0)
            left = jnp.where(jnp.logical_and(inside, c > 0), hbuf[h, 1, rows], 0.0)
            obj[0, 3, rows] = right
            obj[1, 3, rows] = pltpu.roll(right, 64, 1)
            obj[0, 0, rows] = pltpu.roll(left, 64, 1)
            obj[1, 0, rows] = left

        @pl.when(r == 0)
        def _():
            obj[:, 1:3, 0:64] = jnp.zeros((2, 2, 64, WIDTH), F32)

        @pl.when(r == N_ROW - 1)
        def _():
            obj[:, 1:3, 320:384] = jnp.zeros((2, 2, 64, WIDTH), F32)

    def place_of(it, b):
        u = lax.bitwise_and(pos[0, it, 0, 0, b] + shf[0, it, 0, 0, b], TILE - 1)
        w = lax.bitwise_and(pos[1, it, 0, 0, b] + shf[1, it, 0, 0, b], TILE - 1) + HALF
        return u, lax.shift_right_arithmetic(w, 7), lax.bitwise_and(w, 127)

    def patterns(it, first, count):
        pr, pi = prb[0], prb[1]
        ah, al, bh, bl = tab[0], tab[1], tab[2], tab[3]
        patches, shifts_of, stage = [], [], []
        weight = terms[256:384]
        for p in range(count):
            fields = []
            for i in range(2):
                u, k, s = place_of(it, first + 2 * p + i)
                window = lane_full >= s
                parts = []
                for part in range(2):
                    near_block = obj[part, k, pl.ds(u, WIDTH), :]
                    next_block = obj[part, k + 1, pl.ds(u, WIDTH), :]
                    back_by = lax.bitwise_and(WIDTH - s, 127)
                    parts.append(pltpu.roll(jnp.where(window, near_block, next_block), back_by, 1))
                o_re, o_im = parts
                weight = weight + (o_re * o_re + o_im * o_im)
                patches.append((o_re, o_im))
                shifts_of.append(s)
                fields.append((pr * o_re - pi * o_im, pr * o_im + pi * o_re))
            stage.append(
                jnp.concatenate(
                    [
                        jnp.concatenate([fields[0][0], fields[1][0]], axis=1),
                        jnp.concatenate([fields[0][1], fields[1][1]], axis=1),
                    ],
                    axis=0,
                )
            )
        terms[256:384] = weight
        stage = [left_mul(ah, al, v) for v in stage]
        stage = [right_mul(swap_quadrants(v), bh, bl) for v in stage]
        kept = []
        for p, v in enumerate(stage):
            f_re, f_im = v[:, :WIDTH], v[:, WIDTH:]
            measured = amp[it, pl.ds(first + 2 * p, 2)].reshape(2 * WIDTH, WIDTH)
            keep = 1.0 - measured * lax.rsqrt(jnp.maximum(f_re * f_re + f_im * f_im, 1.0))
            kept.append(jnp.concatenate([keep * f_re, keep * f_im], axis=1))
        stage = [right_mul(v, ah, al) for v in kept]
        stage = [left_mul(bh, bl, swap_quadrants(v)) for v in stage]
        q_re, q_im = terms[0:128], terms[128:256]
        for p, v in enumerate(stage):
            for i in range(2):
                b_re = v[:WIDTH, i * WIDTH:(i + 1) * WIDTH]
                b_im = v[WIDTH:, i * WIDTH:(i + 1) * WIDTH]
                o_re, o_im = patches[2 * p + i]
                q_re = q_re + (o_re * b_re + o_im * b_im)
                q_im = q_im + (o_re * b_im - o_im * b_re)
                s = shifts_of[2 * p + i]
                b = first + 2 * p + i
                zb[b, 0, CENTRE:CENTRE + WIDTH] = pltpu.roll(pr * b_re + pi * b_im, s, 1)
                zb[b, 1, CENTRE:CENTRE + WIDTH] = pltpu.roll(pr * b_im - pi * b_re, s, 1)
        terms[0:128] = q_re
        terms[128:256] = q_im

    def gather_gradient(it, j, t):
        def add(b, acc):
            u, k, s = place_of(it, b)
            start = CENTRE - u + 64 * t
            low = jnp.where(k == j, s, WIDTH)
            high = jnp.where(k + 1 == j, s, 0)
            mine = jnp.logical_or(lane >= low, lane < high)
            return tuple(
                acc[part] + jnp.where(mine, zb[b, part, pl.ds(start, 64), :], 0.0) for part in range(2)
            )

        zero = jnp.zeros((64, WIDTH), F32)
        re, im = lax.fori_loop(0, BATCH, add, (zero, zero), unroll=4)
        if isinstance(t, int):
            rows = slice(64 * t, 64 * t + 64)
        else:
            rows = pl.ds(pl.multiple_of(64 * t, 64), 64)
        grad[0, j, rows] = re
        grad[1, j, rows] = im
        return re, im

    def fold_copies(it):
        src = [
            grad.at[:, 1:3, 0:64], grad.at[:, 1:3, 320:384], pack.at[0, 64:320], pack.at[1, 64:320],
            pack.at[0, 0:64], pack.at[1, 0:64], pack.at[0, 320:384], pack.at[1, 320:384],
        ]
        dst = [
            fold_row.at[0], fold_row.at[1], fold_col.at[0], fold_col.at[1],
            fold_cor.at[0], fold_cor.at[1], fold_cor.at[2], fold_cor.at[3],
        ]
        return [
            remote(src[i], dst[i], fold_s.at[it, i], fold_r.at[it, i], near(*around[i])) for i in range(8)
        ]

    def rim(it, t):
        re, im = gather_gradient(it, 0, t)
        rows = slice(64 * t, 64 * t + 64) if isinstance(t, int) else pl.ds(pl.multiple_of(64 * t, 64), 64)
        pack[0, rows] = jnp.where(low_half, pltpu.roll(re, 64, 1), im)
        re, im = gather_gradient(it, 3, t)
        pack[1, rows] = jnp.where(low_half, re, pltpu.roll(im, 64, 1))

    def fold_send(it):
        copies = fold_copies(it)
        for t, i in ((0, 0), (5, 1)):
            gather_gradient(it, 1, t)
            gather_gradient(it, 2, t)
            copies[i].start()
        rim(it, 0)
        copies[4].start()
        copies[5].start()
        rim(it, 5)
        copies[6].start()
        copies[7].start()

        def middle(t, carry):
            rim(it, t)
            return carry

        lax.fori_loop(1, 5, middle, 0)
        copies[2].start()
        copies[3].start()
        return copies

    def interior(it):
        def rows(t, carry):
            gather_gradient(it, 1, t)
            gather_gradient(it, 2, t)
            return carry

        lax.fori_loop(1, 5, rows, 0)

    def fold_finish(copies, step):
        for copy in copies:
            copy.wait()
        up, down, left, right = r > 0, r < N_ROW - 1, c > 0, c < N_COL - 1
        for t in range(4):
            rows = slice(HALF + 64 * t, HALF + 64 * t + 64)
            at = slice(64 * t, 64 * t + 64)
            from_left = jnp.where(left, fold_col[1, at], 0.0)
            from_right = jnp.where(right, fold_col[0, at], 0.0)
            if t == 0:
                from_left = from_left + jnp.where(jnp.logical_and(up, left), fold_cor[3], 0.0)
                from_right = from_right + jnp.where(jnp.logical_and(up, right), fold_cor[2], 0.0)
            if t == 3:
                from_left = from_left + jnp.where(jnp.logical_and(down, left), fold_cor[1], 0.0)
                from_right = from_right + jnp.where(jnp.logical_and(down, right), fold_cor[0], 0.0)
            added = [
                [jnp.where(low_half, from_left, 0.0), jnp.where(low_half, 0.0, pltpu.roll(from_right, 64, 1))],
                [jnp.where(low_half, pltpu.roll(from_left, 64, 1), 0.0), jnp.where(low_half, 0.0, from_right)],
            ]
            for part in range(2):
                for j in (1, 2):
                    g = grad[part, j, rows] + added[part][j - 1]
                    if t == 0:
                        g = g + jnp.where(up, fold_row[1, part, j - 1], 0.0)
                    if t == 3:
                        g = g + jnp.where(down, fold_row[0, part, j - 1], 0.0)
                    obj[part, j, rows] = obj[part, j, rows] - step * g

    half_at = pl.multiple_of(core * CORE_ROWS, 8)
    other_at = pl.multiple_of((1 - core) * CORE_ROWS, 8)

    def core_scatter(it):
        copy = remote(
            terms.at[pl.ds(other_at, CORE_ROWS)], core_buf.at[it], core_s.at[it, 0], core_r.at[it, 0], partner
        )
        copy.start()
        return copy

    def z_scatter(it, before):
        before.wait()
        total[it, pl.ds(half_at, CORE_ROWS)] = terms[pl.ds(half_at, CORE_ROWS)] + core_buf[it]
        copies = []
        for d in range(1, NZ):
            rows = pl.ds(pl.multiple_of(half_at + ((z + d) % NZ) * CHUNK, 8), CHUNK)
            copies.append(remote(total.at[it, rows], z_buf.at[it, d], z_s.at[it, d], z_r.at[it, d], at_z(d)))
            copies[-1].start()
        return copies

    mine_at = pl.multiple_of(half_at + z * CHUNK, 8)

    def xy_gather(it, before):
        for copy in before:
            copy.wait()
        value = total[it, pl.ds(mine_at, CHUNK)]
        for d in range(1, NZ):
            value = value + z_buf[it, d]
        xy_buf[it, xy] = value
        for d in range(1, NX * NY):
            remote(xy_buf.at[it, xy], xy_buf.at[it, xy], xy_s.at[it, d], xy_r.at[it, d], at_xy(d)).start()

    def z_gather(it):
        for d in range(1, NX * NY):
            arriving = (xy + NX * NY - d) % (NX * NY)
            remote(xy_buf.at[it, xy], xy_buf.at[it, arriving], xy_s.at[it, d], xy_r.at[it, d], at_xy(d)).wait()
        value = xy_buf[it, 0]
        for d in range(1, NX * NY):
            value = value + xy_buf[it, d]
        summed[it, pl.ds(mine_at, CHUNK)] = value
        rows = summed.at[it, pl.ds(mine_at, CHUNK)]
        for d in range(1, NZ):
            remote(rows, rows, z_s.at[it, NZ + d], z_r.at[it, NZ + d], at_z(d)).start()

    def core_gather(it):
        rows = summed.at[it, pl.ds(mine_at, CHUNK)]
        for d in range(1, NZ):
            arriving = pl.multiple_of(half_at + ((z + NZ - d) % NZ) * CHUNK, 8)
            remote(
                rows, summed.at[it, pl.ds(arriving, CHUNK)], z_s.at[it, NZ + d], z_r.at[it, NZ + d], at_z(d)
            ).wait()
        half = summed.at[it, pl.ds(half_at, CORE_ROWS)]
        remote(half, half, core_s.at[it, 1], core_r.at[it, 1], partner).start()

    def new_probe_from(it):
        half = summed.at[it, pl.ds(half_at, CORE_ROWS)]
        other = summed.at[it, pl.ds(other_at, CORE_ROWS)]
        remote(half, other, core_s.at[it, 1], core_r.at[it, 1], partner).wait()
        under = summed[it, 256:384] + 0.2 * PATTERNS
        prb[0] = prb[0] - summed[it, 0:128] / under
        prb[1] = prb[1] - summed[it, 128:256] / under

    loads[0].wait()
    loads[1].wait()
    pl.semaphore_wait(barrier, len(peers))
    copies = halo_send(0)

    def clear(b, carry):
        for part in range(2):
            zb[b, part, 0:CENTRE] = jnp.zeros((CENTRE, WIDTH), F32)
            zb[b, part, CENTRE + WIDTH:] = jnp.zeros((PLACED - CENTRE - WIDTH, WIDTH), F32)
        return carry

    lax.fori_loop(0, BATCH, clear, 0)
    loads[2].wait()
    loads[3].wait()
    halo_finish(0, copies)

    for it in range(ITERS):
        terms[...] = jnp.zeros((TERM_ROWS, WIDTH), F32)

        def some(g, carry):
            patterns(it, g * 4, 2)
            return carry

        lax.fori_loop(0, BATCH // 4, some, 0)
        power = prb[0] * prb[0] + prb[1] * prb[1]
        step = 0.5 / (jnp.max(power) + 1e-6)
        summing = core_scatter(it)
        copies = fold_send(it)
        summing = z_scatter(it, summing)
        interior(it)
        xy_gather(it, summing)
        fold_finish(copies, step)
        if it + 1 < ITERS:
            copies = halo_send(it + 1)
        else:
            for j in range(2):
                new_obj[:, :, j * 128:(j + 1) * 128] = obj[:, 1 + j, HALF:HALF + TILE]
        z_gather(it)
        core_gather(it)
        new_probe_from(it)
        if it + 1 < ITERS:
            halo_finish(it + 1, copies)
    new_probe[...] = prb[...]


def local(object_field, probe_field, amplitudes, positions, shifts):
    vmem = pl.BlockSpec(memory_space=pltpu.VMEM)
    smem = pl.BlockSpec(memory_space=pltpu.SMEM)
    hbm = pl.BlockSpec(memory_space=pl.ANY)
    dma = pltpu.SemaphoreType.DMA
    scratch = [
        pltpu.VMEM((2, BLOCKS, PAD, WIDTH), F32),
        pltpu.VMEM((2, WIDTH, WIDTH), F32),
        pltpu.VMEM((ITERS, BATCH, WIDTH, WIDTH), F32),
        pltpu.VMEM((BATCH, 2, PLACED, WIDTH), F32),
        pltpu.VMEM((2, BLOCKS, PAD, WIDTH), F32),
        pltpu.VMEM((TERM_ROWS, WIDTH), F32),
        pltpu.VMEM((2, PAD, WIDTH), F32),
        pltpu.VMEM((2, 2, 2, HALF, WIDTH), F32),
        pltpu.VMEM((2, TILE, WIDTH), F32),
        pltpu.VMEM((4, HALF, WIDTH), F32),
        pltpu.VMEM((ITERS, 2, TILE, WIDTH), F32),
        pltpu.VMEM((ITERS, 2, PAD, WIDTH), F32),
        pltpu.VMEM((ITERS, CORE_ROWS, WIDTH), F32),
        pltpu.VMEM((ITERS, NZ, CHUNK, WIDTH), F32),
        pltpu.VMEM((ITERS, NX * NY, CHUNK, WIDTH), F32),
        pltpu.VMEM((ITERS, TERM_ROWS, WIDTH), F32),
        pltpu.VMEM((ITERS, TERM_ROWS, WIDTH), F32),
        dma((4,)),
        dma((ITERS, 8)), dma((ITERS, 8)),
        dma((ITERS, 8)), dma((ITERS, 8)),
        dma((ITERS, 2)), dma((ITERS, 2)),
        dma((ITERS, 2 * NZ)), dma((ITERS, 2 * NZ)),
        dma((ITERS, NX * NY)), dma((ITERS, NX * NY)),
    ]
    return pl.pallas_call(
        kernel,
        out_shape=(
            jax.ShapeDtypeStruct((2, TILE, TILE), F32),
            jax.ShapeDtypeStruct((2, WIDTH, WIDTH), F32),
        ),
        in_specs=[hbm, hbm, hbm, smem, smem, vmem],
        out_specs=(vmem, vmem),
        scratch_shapes=scratch,
        compiler_params=pltpu.CompilerParams(
            collective_id=0, has_side_effects=True, vmem_limit_bytes=48 * 1024 * 1024
        ),
    )(object_field, probe_field, amplitudes, positions, shifts, jnp.asarray(tables()))


def solution(mesh):
    in_specs = (
        P(None, "row", "col"),
        P(),
        P(None, "row", "col", None, None, None),
        P(None, None, "row", "col", None),
        P(None, None, "row", "col", None),
    )
    out_specs = (P(None, "row", "col"), P())
    return jax.shard_map(local, mesh=mesh, in_specs=in_specs, out_specs=out_specs, check_vma=False)
```

```python
import functools
import math

import jax
import jax.numpy as jnp
import numpy as np
from jax import lax
from jax.experimental import pallas as pl
from jax.experimental.pallas import tpu as pltpu
from jax.sharding import PartitionSpec as P

MESH = pl.DeviceIdType.MESH
F32 = jnp.float32
BF16 = jnp.bfloat16

WIDTH = 128
HALF = 64
TILE = 256
PAD = TILE + 2 * HALF
BLOCKS = 4
BATCH = 16
ITERS = 2
N_ROW = 16
N_COL = 16
NX, NY, NZ = 4, 4, 8
PATTERNS = BATCH * N_ROW * N_COL
TERM_ROWS = 3 * WIDTH
CHUNK = TERM_ROWS // (NX * NY)
CENTRE = 256
PLACED = CENTRE + WIDTH + 256


def tables():
    n = np.arange(WIDTH)
    angle = (np.outer(n, n) % WIDTH) * (2.0 * math.pi / WIDTH)
    c, s = np.cos(angle) / math.sqrt(WIDTH), np.sin(angle) / math.sqrt(WIDTH)
    return np.stack([np.block([[c, s], [-s, c]]), np.block([[c, -s], [s, c]])]).astype(np.float32)


def split(x):
    high = x.astype(BF16)
    return high, (x - high.astype(F32)).astype(BF16)


def mm(a, b):
    return jnp.dot(a, b, preferred_element_type=F32)


def left_mul(high, low, x):
    xh, xl = split(x)
    return mm(high, xh) + mm(high, xl) + mm(low, xh)


def right_mul(x, high, low):
    xh, xl = split(x)
    return mm(xh, high) + mm(xl, high) + mm(xh, low)


def swap_quadrants(y):
    top = jnp.concatenate([y[:WIDTH, :WIDTH], y[WIDTH:, :WIDTH]], axis=1)
    low = jnp.concatenate([y[:WIDTH, WIDTH:], y[WIDTH:, WIDTH:]], axis=1)
    return jnp.concatenate([top, low], axis=0)


def kernel(
    obj_in, probe_in, amp_in, pos_in, shf_in, tab_in, new_obj, new_probe,
    pos, shf, tab32, tab, obj, prb, amp, zb, grad, terms, pack, fold_row, fold_col, fold_cor,
    hpack, hbuf, xy_buf, zc_buf, summed,
    in_sem, halo_s, halo_r, fold_s, fold_r, xy_s, xy_r, zc_s, zc_r, out_s, out_r,
):
    r, c = lax.axis_index("row"), lax.axis_index("col")
    y, zh, core = r // 4, (r // 2) % 2, r % 2
    zl, x = c // 4, c % 4
    zc = (zh * 4 + zl) * 2 + core
    xy = y * NX + x

    def near(dr, dc):
        return ((r + dr + N_ROW) % N_ROW, (c + dc + N_COL) % N_COL)

    def at_zc(d):
        other = (zc + d) % (2 * NZ)
        return (y * 4 + (other // 8) * 2 + other % 2, ((other // 2) % 4) * 4 + x)

    def at_xy(d):
        other = (xy + d) % (NX * NY)
        return ((other // NX) * 4 + zh * 2 + core, zl * 4 + other % NX)

    around = [(-1, 0), (1, 0), (0, -1), (0, 1), (-1, -1), (-1, 1), (1, -1), (1, 1), (-1, 0), (1, 0)]

    barrier = pltpu.get_barrier_semaphore()
    peers = [near(*d) for d in around[:8]]
    peers += [at_zc(d) for d in range(1, 2 * NZ)] + [at_xy(d) for d in range(1, NX * NY)]
    for peer in peers:
        pl.semaphore_signal(barrier, inc=1, device_id=peer, device_id_type=MESH)

    loads = [
        pltpu.make_async_copy(obj_in.at[:, :, 0:128], obj.at[:, 1, HALF:HALF + TILE], in_sem.at[0]),
        pltpu.make_async_copy(obj_in.at[:, :, 128:256], obj.at[:, 2, HALF:HALF + TILE], in_sem.at[1]),
        pltpu.make_async_copy(probe_in, prb, in_sem.at[2]),
        pltpu.make_async_copy(pos_in, pos, in_sem.at[3]),
        pltpu.make_async_copy(shf_in, shf, in_sem.at[4]),
        pltpu.make_async_copy(tab_in, tab32, in_sem.at[5]),
        pltpu.make_async_copy(amp_in.at[:, 0, 0], amp, in_sem.at[6]),
    ]
    for load in loads:
        load.start()

    lane = lax.broadcasted_iota(jnp.int32, (HALF, WIDTH), 1)
    lane_full = lax.broadcasted_iota(jnp.int32, (WIDTH, WIDTH), 1)
    low_half = lane < HALF

    def remote(src, dst, ss, rs, to):
        return pltpu.make_async_remote_copy(
            src_ref=src, dst_ref=dst, send_sem=ss, recv_sem=rs, device_id=to, device_id_type=MESH
        )

    def halo_copies(h):
        src = [
            obj.at[:, 1, 64:128], obj.at[:, 1, 256:320], hpack.at[h, 0], hpack.at[h, 1],
            hpack.at[h, 0, 0:64], hpack.at[h, 1, 0:64], hpack.at[h, 0, 192:256], hpack.at[h, 1, 192:256],
            obj.at[:, 2, 64:128], obj.at[:, 2, 256:320],
        ]
        dst = [
            obj.at[:, 1, 320:384], obj.at[:, 1, 0:64], hbuf.at[h, 0, 64:320], hbuf.at[h, 1, 64:320],
            hbuf.at[h, 0, 320:384], hbuf.at[h, 1, 320:384], hbuf.at[h, 0, 0:64], hbuf.at[h, 1, 0:64],
            obj.at[:, 2, 320:384], obj.at[:, 2, 0:64],
        ]
        return [
            remote(src[i], dst[i], halo_s.at[h, i], halo_r.at[h, i], near(*around[i])) for i in range(10)
        ]

    def halo_send(h, copies, j):
        for t in (0, 3, 1, 2):
            rows = slice(HALF + 64 * t, HALF + 64 * t + 64)
            to = slice(64 * t, 64 * t + 64)
            re, im = obj[0, j, rows], obj[1, j, rows]
            if j == 1:
                hpack[h, 0, to] = jnp.where(low_half, re, pltpu.roll(im, 64, 1))
            else:
                hpack[h, 1, to] = jnp.where(low_half, pltpu.roll(re, 64, 1), im)
            if t == 3:
                for i in (4, 6, 0, 1) if j == 1 else (5, 7, 8, 9):
                    copies[i].start()
        copies[2 if j == 1 else 3].start()

    def halo_finish(h, copies):
        for copy in copies:
            copy.wait()
        for t in range(6):
            rows = slice(64 * t, 64 * t + 64)
            inside = r >= 0
            if t == 0:
                inside = r > 0
            if t == 5:
                inside = r < N_ROW - 1
            right = jnp.where(jnp.logical_and(inside, c < N_COL - 1), hbuf[h, 0, rows], 0.0)
            left = jnp.where(jnp.logical_and(inside, c > 0), hbuf[h, 1, rows], 0.0)
            obj[0, 3, rows] = right
            obj[1, 3, rows] = pltpu.roll(right, 64, 1)
            obj[0, 0, rows] = pltpu.roll(left, 64, 1)
            obj[1, 0, rows] = left

        @pl.when(r == 0)
        def _():
            obj[:, 1:3, 0:64] = jnp.zeros((2, 2, 64, WIDTH), F32)

        @pl.when(r == N_ROW - 1)
        def _():
            obj[:, 1:3, 320:384] = jnp.zeros((2, 2, 64, WIDTH), F32)

    def place_of(it, b):
        u = lax.bitwise_and(pos[0, it, 0, 0, b] + shf[0, it, 0, 0, b], TILE - 1)
        w = lax.bitwise_and(pos[1, it, 0, 0, b] + shf[1, it, 0, 0, b], TILE - 1) + HALF
        return u, lax.shift_right_arithmetic(w, 7), lax.bitwise_and(w, 127)

    def patterns(it, first, count):
        pr, pi = prb[0], prb[1]
        ah, al, bh, bl = tab[0], tab[1], tab[2], tab[3]
        patches, shifts_of, stage = [], [], []
        weight = terms[256:384]
        for p in range(count):
            fields = []
            for i in range(2):
                u, k, s = place_of(it, first + 2 * p + i)
                window = lane_full >= s
                parts = []
                for part in range(2):
                    near_block = obj[part, k, pl.ds(u, WIDTH), :]
                    next_block = obj[part, k + 1, pl.ds(u, WIDTH), :]
                    back_by = lax.bitwise_and(WIDTH - s, 127)
                    parts.append(pltpu.roll(jnp.where(window, near_block, next_block), back_by, 1))
                o_re, o_im = parts
                weight = weight + (o_re * o_re + o_im * o_im)
                patches.append((o_re, o_im))
                shifts_of.append(s)
                fields.append((pr * o_re - pi * o_im, pr * o_im + pi * o_re))
            stage.append(
                jnp.concatenate(
                    [
                        jnp.concatenate([fields[0][0], fields[1][0]], axis=1),
                        jnp.concatenate([fields[0][1], fields[1][1]], axis=1),
                    ],
                    axis=0,
                )
            )
        terms[256:384] = weight
        stage = [left_mul(ah, al, v) for v in stage]
        stage = [right_mul(swap_quadrants(v), bh, bl) for v in stage]
        kept = []
        for p, v in enumerate(stage):
            f_re, f_im = v[:, :WIDTH], v[:, WIDTH:]
            measured = amp[it, pl.ds(first + 2 * p, 2)].reshape(2 * WIDTH, WIDTH)
            keep = 1.0 - measured * lax.rsqrt(jnp.maximum(f_re * f_re + f_im * f_im, 1.0))
            kept.append(jnp.concatenate([keep * f_re, keep * f_im], axis=1))
        stage = [right_mul(v, ah, al) for v in kept]
        stage = [left_mul(bh, bl, swap_quadrants(v)) for v in stage]
        q_re, q_im = terms[0:128], terms[128:256]
        for p, v in enumerate(stage):
            for i in range(2):
                b_re = v[:WIDTH, i * WIDTH:(i + 1) * WIDTH]
                b_im = v[WIDTH:, i * WIDTH:(i + 1) * WIDTH]
                o_re, o_im = patches[2 * p + i]
                q_re = q_re + (o_re * b_re + o_im * b_im)
                q_im = q_im + (o_re * b_im - o_im * b_re)
                s = shifts_of[2 * p + i]
                b = first + 2 * p + i
                zb[b, 0, CENTRE:CENTRE + WIDTH] = pltpu.roll(pr * b_re + pi * b_im, s, 1)
                zb[b, 1, CENTRE:CENTRE + WIDTH] = pltpu.roll(pr * b_im - pi * b_re, s, 1)
        terms[0:128] = q_re
        terms[128:256] = q_im

    def gather_gradient(it, j, t):
        def add(b, acc):
            u, k, s = place_of(it, b)
            start = CENTRE - u + 64 * t
            low = jnp.where(k == j, s, WIDTH)
            high = jnp.where(k + 1 == j, s, 0)
            mine = jnp.logical_or(lane >= low, lane < high)
            return tuple(
                acc[part] + jnp.where(mine, zb[b, part, pl.ds(start, 64), :], 0.0) for part in range(2)
            )

        zero = jnp.zeros((64, WIDTH), F32)
        re, im = lax.fori_loop(0, BATCH, add, (zero, zero), unroll=4)
        if isinstance(t, int):
            rows = slice(64 * t, 64 * t + 64)
        else:
            rows = pl.ds(pl.multiple_of(64 * t, 64), 64)
        grad[0, j, rows] = re
        grad[1, j, rows] = im
        return re, im

    def fold_copies(it):
        src = [
            grad.at[:, 1, 0:64], grad.at[:, 1, 320:384], pack.at[0, 64:320], pack.at[1, 64:320],
            pack.at[0, 0:64], pack.at[1, 0:64], pack.at[0, 320:384], pack.at[1, 320:384],
            grad.at[:, 2, 0:64], grad.at[:, 2, 320:384],
        ]
        dst = [
            fold_row.at[0, 0], fold_row.at[1, 0], fold_col.at[0], fold_col.at[1],
            fold_cor.at[0], fold_cor.at[1], fold_cor.at[2], fold_cor.at[3],
            fold_row.at[0, 1], fold_row.at[1, 1],
        ]
        return [
            remote(src[i], dst[i], fold_s.at[it, i], fold_r.at[it, i], near(*around[i])) for i in range(10)
        ]

    def rim(it, t):
        re, im = gather_gradient(it, 0, t)
        rows = slice(64 * t, 64 * t + 64) if isinstance(t, int) else pl.ds(pl.multiple_of(64 * t, 64), 64)
        pack[0, rows] = jnp.where(low_half, pltpu.roll(re, 64, 1), im)
        re, im = gather_gradient(it, 3, t)
        pack[1, rows] = jnp.where(low_half, re, pltpu.roll(im, 64, 1))

    def fold_send(it):
        copies = fold_copies(it)
        for t, corners in ((0, (4, 5)), (5, (6, 7))):
            rim(it, t)
            for i in corners:
                copies[i].start()
        for j in (1, 2):
            for t in (0, 5):
                gather_gradient(it, j, t)
                copies[(0 if j == 1 else 8) + t // 5].start()

        def middle(t, carry):
            rim(it, t)
            return carry

        lax.fori_loop(1, 5, middle, 0)
        copies[2].start()
        copies[3].start()
        return copies

    def interior(it):
        def rows(t, carry):
            gather_gradient(it, 1, t)
            gather_gradient(it, 2, t)
            return carry

        lax.fori_loop(1, 5, rows, 0)

    def fold_finish(copies, step, j):
        for i in (0, 1, 3, 5, 7) if j == 1 else (8, 9, 2, 4, 6):
            copies[i].wait()
        up, down = r > 0, r < N_ROW - 1
        beside = c > 0 if j == 1 else c < N_COL - 1
        for t in range(4):
            rows = slice(HALF + 64 * t, HALF + 64 * t + 64)
            at = slice(64 * t, 64 * t + 64)
            side = jnp.where(beside, fold_col[2 - j if j == 2 else 1, at], 0.0)
            if t == 0:
                side = side + jnp.where(jnp.logical_and(up, beside), fold_cor[3 if j == 1 else 2], 0.0)
            if t == 3:
                side = side + jnp.where(jnp.logical_and(down, beside), fold_cor[1 if j == 1 else 0], 0.0)
            if j == 1:
                added = [jnp.where(low_half, side, 0.0), jnp.where(low_half, pltpu.roll(side, 64, 1), 0.0)]
            else:
                added = [jnp.where(low_half, 0.0, pltpu.roll(side, 64, 1)), jnp.where(low_half, 0.0, side)]
            for part in range(2):
                g = grad[part, j, rows] + added[part]
                if t == 0:
                    g = g + jnp.where(up, fold_row[1, j - 1, part], 0.0)
                if t == 3:
                    g = g + jnp.where(down, fold_row[0, j - 1, part], 0.0)
                obj[part, j, rows] = obj[part, j, rows] - step * g

    def chunk(i):
        return pl.ds(pl.multiple_of(i * CHUNK, 8), CHUNK)

    def xy_scatter(it):
        copies = []
        for d in range(1, NX * NY):
            copies.append(
                remote(
                    terms.at[chunk((xy + d) % (NX * NY))], xy_buf.at[it, d],
                    xy_s.at[it, d], xy_r.at[it, d], at_xy(d),
                )
            )
            copies[-1].start()
        return copies

    def zc_gather(it, before):
        for copy in before:
            copy.wait()
        value = terms[chunk(xy)]
        for d in range(1, NX * NY):
            value = value + xy_buf[it, d]
        zc_buf[it, zc] = value
        for d in range(1, 2 * NZ):
            remote(zc_buf.at[it, zc], zc_buf.at[it, zc], zc_s.at[it, d], zc_r.at[it, d], at_zc(d)).start()

    def xy_gather(it):
        for d in range(1, 2 * NZ):
            arriving = zc_buf.at[it, (zc + 2 * NZ - d) % (2 * NZ)]
            remote(zc_buf.at[it, zc], arriving, zc_s.at[it, d], zc_r.at[it, d], at_zc(d)).wait()
        value = zc_buf[it, 0]
        for d in range(1, 2 * NZ):
            value = value + zc_buf[it, d]
        summed[it, chunk(xy)] = value
        rows = summed.at[it, chunk(xy)]
        for d in range(1, NX * NY):
            remote(rows, rows, out_s.at[it, d], out_r.at[it, d], at_xy(d)).start()

    def new_probe_from(it):
        rows = summed.at[it, chunk(xy)]
        for d in range(1, NX * NY):
            arriving = summed.at[it, chunk((xy + NX * NY - d) % (NX * NY))]
            remote(rows, arriving, out_s.at[it, d], out_r.at[it, d], at_xy(d)).wait()
        under = summed[it, 256:384] + 0.2 * PATTERNS
        prb[0] = prb[0] - summed[it, 0:128] / under
        prb[1] = prb[1] - summed[it, 128:256] / under

    loads[0].wait()
    loads[1].wait()
    pl.semaphore_wait(barrier, len(peers))
    copies = halo_copies(0)
    halo_send(0, copies, 1)
    halo_send(0, copies, 2)

    def clear(b, carry):
        for part in range(2):
            zb[b, part, 0:CENTRE] = jnp.zeros((CENTRE, WIDTH), F32)
            zb[b, part, CENTRE + WIDTH:] = jnp.zeros((PLACED - CENTRE - WIDTH, WIDTH), F32)
        return carry

    lax.fori_loop(0, BATCH, clear, 0)
    for load in loads[2:]:
        load.wait()
    for m in range(2):
        tab[2 * m], tab[2 * m + 1] = split(tab32[m])
    halo_finish(0, copies)

    for it in range(ITERS):
        terms[...] = jnp.zeros((TERM_ROWS, WIDTH), F32)

        def some(g, carry):
            patterns(it, g * 4, 2)
            return carry

        lax.fori_loop(0, BATCH // 4, some, 0)
        power = prb[0] * prb[0] + prb[1] * prb[1]
        step = 0.5 / (jnp.max(power) + 1e-6)
        summing = xy_scatter(it)
        folds = fold_send(it)
        interior(it)
        zc_gather(it, summing)
        if it + 1 < ITERS:
            copies = halo_copies(it + 1)
        else:
            stores = [
                pltpu.make_async_copy(
                    obj.at[:, 1 + j, HALF:HALF + TILE], new_obj.at[:, :, j * 128:(j + 1) * 128], in_sem.at[7 + j]
                )
                for j in range(2)
            ]
        for j in (1, 2):
            fold_finish(folds, step, j)
            if it + 1 < ITERS:
                halo_send(it + 1, copies, j)
            else:
                stores[j - 1].start()
        xy_gather(it)
        new_probe_from(it)
        if it + 1 < ITERS:
            halo_finish(it + 1, copies)
    stores.append(pltpu.make_async_copy(prb, new_probe, in_sem.at[9]))
    stores[2].start()
    for store in stores:
        store.wait()


def local(object_field, probe_field, amplitudes, positions, shifts):
    hbm = pl.BlockSpec(memory_space=pltpu.HBM)
    dma = pltpu.SemaphoreType.DMA
    scratch = [
        pltpu.SMEM(positions.shape, jnp.int32),
        pltpu.SMEM(shifts.shape, jnp.int32),
        pltpu.VMEM((2, 2 * WIDTH, 2 * WIDTH), F32),
        pltpu.VMEM((4, 2 * WIDTH, 2 * WIDTH), BF16),
        pltpu.VMEM((2, BLOCKS, PAD, WIDTH), F32),
        pltpu.VMEM((2, WIDTH, WIDTH), F32),
        pltpu.VMEM((ITERS, BATCH, WIDTH, WIDTH), F32),
        pltpu.VMEM((BATCH, 2, PLACED, WIDTH), F32),
        pltpu.VMEM((2, BLOCKS, PAD, WIDTH), F32),
        pltpu.VMEM((TERM_ROWS, WIDTH), F32),
        pltpu.VMEM((2, PAD, WIDTH), F32),
        pltpu.VMEM((2, 2, 2, HALF, WIDTH), F32),
        pltpu.VMEM((2, TILE, WIDTH), F32),
        pltpu.VMEM((4, HALF, WIDTH), F32),
        pltpu.VMEM((ITERS, 2, TILE, WIDTH), F32),
        pltpu.VMEM((ITERS, 2, PAD, WIDTH), F32),
        pltpu.VMEM((ITERS, NX * NY, CHUNK, WIDTH), F32),
        pltpu.VMEM((ITERS, 2 * NZ, CHUNK, WIDTH), F32),
        pltpu.VMEM((ITERS, TERM_ROWS, WIDTH), F32),
        dma((10,)),
        dma((ITERS, 10)), dma((ITERS, 10)),
        dma((ITERS, 10)), dma((ITERS, 10)),
        dma((ITERS, NX * NY)), dma((ITERS, NX * NY)),
        dma((ITERS, 2 * NZ)), dma((ITERS, 2 * NZ)),
        dma((ITERS, NX * NY)), dma((ITERS, NX * NY)),
    ]
    return pl.pallas_call(
        kernel,
        out_shape=(
            jax.ShapeDtypeStruct((2, TILE, TILE), F32),
            jax.ShapeDtypeStruct((2, WIDTH, WIDTH), F32),
        ),
        in_specs=[hbm] * 6,
        out_specs=(hbm, hbm),
        scratch_shapes=scratch,
        compiler_params=pltpu.CompilerParams(
            collective_id=0, has_side_effects=True, vmem_limit_bytes=60 * 1024 * 1024
        ),
    )(object_field, probe_field, amplitudes, positions, shifts, jnp.asarray(tables()))


def solution(mesh):
    in_specs = (
        P(None, "row", "col"),
        P(),
        P(None, "row", "col", None, None, None),
        P(None, None, "row", "col", None),
        P(None, None, "row", "col", None),
    )
    out_specs = (P(None, "row", "col"), P())
    return jax.shard_map(local, mesh=mesh, in_specs=in_specs, out_specs=out_specs, check_vma=False)
```

```python
import functools
import math

import jax
import jax.numpy as jnp
import numpy as np
from jax import lax
from jax.experimental import pallas as pl
from jax.experimental.pallas import tpu as pltpu
from jax.sharding import PartitionSpec as P

MESH = pl.DeviceIdType.MESH
F32 = jnp.float32
BF16 = jnp.bfloat16

WIDTH = 128
HALF = 64
TILE = 256
PAD = TILE + 2 * HALF
BLOCKS = 4
BATCH = 16
ITERS = 2
N_ROW = 16
N_COL = 16
NX, NY, NZ = 4, 4, 8
PATTERNS = BATCH * N_ROW * N_COL
TERM_ROWS = 3 * WIDTH
CHUNK = TERM_ROWS // (NX * NY)
CENTRE = 256
PLACED = CENTRE + WIDTH + 256


def tables():
    n = np.arange(WIDTH)
    angle = (np.outer(n, n) % WIDTH) * (2.0 * math.pi / WIDTH)
    c, s = np.cos(angle) / math.sqrt(WIDTH), np.sin(angle) / math.sqrt(WIDTH)
    return np.stack([np.block([[c, s], [-s, c]]), np.block([[c, -s], [s, c]])]).astype(np.float32)


def split(x):
    high = x.astype(BF16)
    return high, (x - high.astype(F32)).astype(BF16)


def mm(a, b):
    return jnp.dot(a, b, preferred_element_type=F32)


def left_mul(high, low, x):
    xh, xl = split(x)
    return mm(high, xh) + mm(high, xl) + mm(low, xh)


def right_mul(x, high, low):
    xh, xl = split(x)
    return mm(xh, high) + mm(xl, high) + mm(xh, low)


def swap_quadrants(y):
    top = jnp.concatenate([y[:WIDTH, :WIDTH], y[WIDTH:, :WIDTH]], axis=1)
    low = jnp.concatenate([y[:WIDTH, WIDTH:], y[WIDTH:, WIDTH:]], axis=1)
    return jnp.concatenate([top, low], axis=0)


def kernel(
    obj_in, probe_in, amp_in, pos_in, shf_in, tab_in, new_obj, new_probe,
    pos, shf, tab32, tab, obj, prb, amp, zb, grad, terms, pack, fold_row, fold_col, fold_cor,
    hpack, hbuf, xy_buf, pair_buf, z_buf, summed,
    in_sem, halo_s, halo_r, fold_s, fold_r, xy_s, xy_r, pair_s, pair_r, z_s, z_r, out_s, out_r,
):
    r, c = lax.axis_index("row"), lax.axis_index("col")
    y, zh, core = r // 4, (r // 2) % 2, r % 2
    zl, x = c // 4, c % 4
    z = zh * 4 + zl
    xy = y * NX + x

    def near(dr, dc):
        return ((r + dr + N_ROW) % N_ROW, (c + dc + N_COL) % N_COL)

    def at_z(d):
        other = (z + d) % NZ
        return (y * 4 + (other // 4) * 2 + core, (other % 4) * 4 + x)

    def at_xy(d):
        other = (xy + d) % (NX * NY)
        return ((other // NX) * 4 + zh * 2 + core, zl * 4 + other % NX)

    partner = (r + 1 - 2 * core, c)
    around = [(-1, 0), (1, 0), (0, -1), (0, 1), (-1, -1), (-1, 1), (1, -1), (1, 1), (-1, 0), (1, 0)]

    barrier = pltpu.get_barrier_semaphore()
    peers = [near(*d) for d in around[:8]]
    peers += [partner] + [at_z(d) for d in range(1, NZ)] + [at_xy(d) for d in range(1, NX * NY)]
    for peer in peers:
        pl.semaphore_signal(barrier, inc=1, device_id=peer, device_id_type=MESH)

    loads = [
        pltpu.make_async_copy(obj_in.at[:, :, 0:128], obj.at[:, 1, HALF:HALF + TILE], in_sem.at[0]),
        pltpu.make_async_copy(obj_in.at[:, :, 128:256], obj.at[:, 2, HALF:HALF + TILE], in_sem.at[1]),
        pltpu.make_async_copy(probe_in, prb, in_sem.at[2]),
        pltpu.make_async_copy(pos_in, pos, in_sem.at[3]),
        pltpu.make_async_copy(shf_in, shf, in_sem.at[4]),
        pltpu.make_async_copy(tab_in, tab32, in_sem.at[5]),
        pltpu.make_async_copy(amp_in.at[:, 0, 0], amp, in_sem.at[6]),
    ]
    for load in loads:
        load.start()

    lane = lax.broadcasted_iota(jnp.int32, (HALF, WIDTH), 1)
    lane_full = lax.broadcasted_iota(jnp.int32, (WIDTH, WIDTH), 1)
    low_half = lane < HALF

    def remote(src, dst, ss, rs, to):
        return pltpu.make_async_remote_copy(
            src_ref=src, dst_ref=dst, send_sem=ss, recv_sem=rs, device_id=to, device_id_type=MESH
        )

    def inside(dr, dc):
        has = [r > 0] if dr < 0 else [r < N_ROW - 1] if dr > 0 else []
        has += [c > 0] if dc < 0 else [c < N_COL - 1] if dc > 0 else []
        return has[0] if len(has) == 1 else jnp.logical_and(*has)

    def start(copies, which):
        for i in which:

            @pl.when(inside(*around[i]))
            def _(copy=copies[i]):
                copy.start()

    def finish(copies, which):
        for i in which:
            dr, dc = around[i]

            @pl.when(inside(dr, dc))
            def _(copy=copies[i]):
                copy.wait_send()

            @pl.when(inside(-dr, -dc))
            def _(copy=copies[i]):
                copy.wait_recv()

    def halo_copies(h):
        src = [
            obj.at[:, 1, 64:128], obj.at[:, 1, 256:320], hpack.at[h, 0], hpack.at[h, 1],
            hpack.at[h, 0, 0:64], hpack.at[h, 1, 0:64], hpack.at[h, 0, 192:256], hpack.at[h, 1, 192:256],
            obj.at[:, 2, 64:128], obj.at[:, 2, 256:320],
        ]
        dst = [
            obj.at[:, 1, 320:384], obj.at[:, 1, 0:64], hbuf.at[h, 0, 64:320], hbuf.at[h, 1, 64:320],
            hbuf.at[h, 0, 320:384], hbuf.at[h, 1, 320:384], hbuf.at[h, 0, 0:64], hbuf.at[h, 1, 0:64],
            obj.at[:, 2, 320:384], obj.at[:, 2, 0:64],
        ]
        return [
            remote(src[i], dst[i], halo_s.at[h, i], halo_r.at[h, i], near(*around[i])) for i in range(10)
        ]

    def halo_send(h, copies, j):
        for t in (0, 3, 1, 2):
            rows = slice(HALF + 64 * t, HALF + 64 * t + 64)
            to = slice(64 * t, 64 * t + 64)
            re, im = obj[0, j, rows], obj[1, j, rows]
            if j == 1:
                hpack[h, 0, to] = jnp.where(low_half, re, pltpu.roll(im, 64, 1))
            else:
                hpack[h, 1, to] = jnp.where(low_half, pltpu.roll(re, 64, 1), im)
            if t == 3:
                start(copies, (4, 6, 0, 1) if j == 1 else (5, 7, 8, 9))
        start(copies, (2,) if j == 1 else (3,))

    def halo_finish(h, copies):
        finish(copies, range(10))
        for t in range(6):
            rows = slice(64 * t, 64 * t + 64)
            dr = -1 if t == 0 else 1 if t == 5 else 0
            right = jnp.where(inside(dr, 1), hbuf[h, 0, rows], 0.0)
            left = jnp.where(inside(dr, -1), hbuf[h, 1, rows], 0.0)
            obj[0, 3, rows] = right
            obj[1, 3, rows] = pltpu.roll(right, 64, 1)
            obj[0, 0, rows] = pltpu.roll(left, 64, 1)
            obj[1, 0, rows] = left

        @pl.when(r == 0)
        def _():
            obj[:, 1:3, 0:64] = jnp.zeros((2, 2, 64, WIDTH), F32)

        @pl.when(r == N_ROW - 1)
        def _():
            obj[:, 1:3, 320:384] = jnp.zeros((2, 2, 64, WIDTH), F32)

    def place_of(it, b):
        u = lax.bitwise_and(pos[0, it, 0, 0, b] + shf[0, it, 0, 0, b], TILE - 1)
        w = lax.bitwise_and(pos[1, it, 0, 0, b] + shf[1, it, 0, 0, b], TILE - 1) + HALF
        return u, lax.shift_right_arithmetic(w, 7), lax.bitwise_and(w, 127)

    def patterns(it, first, count):
        pr, pi = prb[0], prb[1]
        ah, al, bh, bl = tab[0], tab[1], tab[2], tab[3]
        patches, shifts_of, stage = [], [], []
        weight = terms[256:384]
        for p in range(count):
            fields = []
            for i in range(2):
                u, k, s = place_of(it, first + 2 * p + i)
                window = lane_full >= s
                parts = []
                for part in range(2):
                    near_block = obj[part, k, pl.ds(u, WIDTH), :]
                    next_block = obj[part, k + 1, pl.ds(u, WIDTH), :]
                    back_by = lax.bitwise_and(WIDTH - s, 127)
                    parts.append(pltpu.roll(jnp.where(window, near_block, next_block), back_by, 1))
                o_re, o_im = parts
                weight = weight + (o_re * o_re + o_im * o_im)
                patches.append((o_re, o_im))
                shifts_of.append(s)
                fields.append((pr * o_re - pi * o_im, pr * o_im + pi * o_re))
            stage.append(
                jnp.concatenate(
                    [
                        jnp.concatenate([fields[0][0], fields[1][0]], axis=1),
                        jnp.concatenate([fields[0][1], fields[1][1]], axis=1),
                    ],
                    axis=0,
                )
            )
        terms[256:384] = weight
        stage = [left_mul(ah, al, v) for v in stage]
        stage = [right_mul(swap_quadrants(v), bh, bl) for v in stage]
        kept = []
        for p, v in enumerate(stage):
            f_re, f_im = v[:, :WIDTH], v[:, WIDTH:]
            measured = amp[it, pl.ds(first + 2 * p, 2)].reshape(2 * WIDTH, WIDTH)
            keep = 1.0 - measured * lax.rsqrt(jnp.maximum(f_re * f_re + f_im * f_im, 1.0))
            kept.append(jnp.concatenate([keep * f_re, keep * f_im], axis=1))
        stage = [right_mul(v, ah, al) for v in kept]
        stage = [left_mul(bh, bl, swap_quadrants(v)) for v in stage]
        q_re, q_im = terms[0:128], terms[128:256]
        for p, v in enumerate(stage):
            for i in range(2):
                b_re = v[:WIDTH, i * WIDTH:(i + 1) * WIDTH]
                b_im = v[WIDTH:, i * WIDTH:(i + 1) * WIDTH]
                o_re, o_im = patches[2 * p + i]
                q_re = q_re + (o_re * b_re + o_im * b_im)
                q_im = q_im + (o_re * b_im - o_im * b_re)
                s = shifts_of[2 * p + i]
                b = first + 2 * p + i
                zb[b, 0, CENTRE:CENTRE + WIDTH] = pltpu.roll(pr * b_re + pi * b_im, s, 1)
                zb[b, 1, CENTRE:CENTRE + WIDTH] = pltpu.roll(pr * b_im - pi * b_re, s, 1)
        terms[0:128] = q_re
        terms[128:256] = q_im

    def gather_gradient(it, j, t):
        def add(b, acc):
            u, k, s = place_of(it, b)
            start = CENTRE - u + 64 * t
            low = jnp.where(k == j, s, WIDTH)
            high = jnp.where(k + 1 == j, s, 0)
            mine = jnp.logical_or(lane >= low, lane < high)
            return tuple(
                acc[part] + jnp.where(mine, zb[b, part, pl.ds(start, 64), :], 0.0) for part in range(2)
            )

        zero = jnp.zeros((64, WIDTH), F32)
        re, im = lax.fori_loop(0, BATCH, add, (zero, zero), unroll=4)
        if isinstance(t, int):
            rows = slice(64 * t, 64 * t + 64)
        else:
            rows = pl.ds(pl.multiple_of(64 * t, 64), 64)
        grad[0, j, rows] = re
        grad[1, j, rows] = im
        return re, im

    def fold_copies(it):
        src = [
            grad.at[:, 1, 0:64], grad.at[:, 1, 320:384], pack.at[0, 64:320], pack.at[1, 64:320],
            pack.at[0, 0:64], pack.at[1, 0:64], pack.at[0, 320:384], pack.at[1, 320:384],
            grad.at[:, 2, 0:64], grad.at[:, 2, 320:384],
        ]
        dst = [
            fold_row.at[0, 0], fold_row.at[1, 0], fold_col.at[0], fold_col.at[1],
            fold_cor.at[0], fold_cor.at[1], fold_cor.at[2], fold_cor.at[3],
            fold_row.at[0, 1], fold_row.at[1, 1],
        ]
        return [
            remote(src[i], dst[i], fold_s.at[it, i], fold_r.at[it, i], near(*around[i])) for i in range(10)
        ]

    def rim(it, t):
        re, im = gather_gradient(it, 0, t)
        rows = slice(64 * t, 64 * t + 64) if isinstance(t, int) else pl.ds(pl.multiple_of(64 * t, 64), 64)
        pack[0, rows] = jnp.where(low_half, pltpu.roll(re, 64, 1), im)
        re, im = gather_gradient(it, 3, t)
        pack[1, rows] = jnp.where(low_half, re, pltpu.roll(im, 64, 1))

    def fold_send(it):
        copies = fold_copies(it)
        for t, corners in ((0, (4, 5)), (5, (6, 7))):
            rim(it, t)
            start(copies, corners)
        for j in (1, 2):
            for t in (0, 5):
                gather_gradient(it, j, t)
                start(copies, [(0 if j == 1 else 8) + t // 5])

        def middle(t, carry):
            rim(it, t)
            return carry

        lax.fori_loop(1, 5, middle, 0)
        if it + 1 < ITERS:
            start(copies, (2, 3))
        return copies

    def interior(it):
        def rows(t, carry):
            gather_gradient(it, 1, t)
            gather_gradient(it, 2, t)
            return carry

        lax.fori_loop(1, 5, rows, 0)

    def fold_finish(copies, step, j):
        finish(copies, (0, 1, 3, 5, 7) if j == 1 else (8, 9, 2, 4, 6))
        up, down = inside(-1, 0), inside(1, 0)
        beside = inside(0, -1 if j == 1 else 1)
        for t in range(4):
            rows = slice(HALF + 64 * t, HALF + 64 * t + 64)
            at = slice(64 * t, 64 * t + 64)
            side = jnp.where(beside, fold_col[2 - j if j == 2 else 1, at], 0.0)
            if t == 0:
                side = side + jnp.where(jnp.logical_and(up, beside), fold_cor[3 if j == 1 else 2], 0.0)
            if t == 3:
                side = side + jnp.where(jnp.logical_and(down, beside), fold_cor[1 if j == 1 else 0], 0.0)
            if j == 1:
                added = [jnp.where(low_half, side, 0.0), jnp.where(low_half, pltpu.roll(side, 64, 1), 0.0)]
            else:
                added = [jnp.where(low_half, 0.0, pltpu.roll(side, 64, 1)), jnp.where(low_half, 0.0, side)]
            for part in range(2):
                g = grad[part, j, rows] + added[part]
                if t == 0:
                    g = g + jnp.where(up, fold_row[1, j - 1, part], 0.0)
                if t == 3:
                    g = g + jnp.where(down, fold_row[0, j - 1, part], 0.0)
                obj[part, j, rows] = obj[part, j, rows] - step * g

    def chunk(i):
        return pl.ds(pl.multiple_of(i * CHUNK, 8), CHUNK)

    def xy_scatter(it):
        copies = []
        for d in range(1, NX * NY):
            copies.append(
                remote(
                    terms.at[chunk((xy + d) % (NX * NY))], xy_buf.at[it, d],
                    xy_s.at[it, d], xy_r.at[it, d], at_xy(d),
                )
            )
            copies[-1].start()
        return copies

    def z_gather(it, before):
        for copy in before:
            copy.wait()
        value = terms[chunk(xy)]
        for d in range(1, NX * NY):
            value = value + xy_buf[it, d]
        pair_buf[it, 0] = value
        swap = remote(pair_buf.at[it, 0], pair_buf.at[it, 1], pair_s.at[it], pair_r.at[it], partner)
        swap.start()
        swap.wait()
        z_buf[it, z] = value + pair_buf[it, 1]
        for d in range(1, NZ):
            remote(z_buf.at[it, z], z_buf.at[it, z], z_s.at[it, d], z_r.at[it, d], at_z(d)).start()

    def xy_gather(it):
        for d in range(1, NZ):
            arriving = z_buf.at[it, (z + NZ - d) % NZ]
            remote(z_buf.at[it, z], arriving, z_s.at[it, d], z_r.at[it, d], at_z(d)).wait()
        value = z_buf[it, 0]
        for d in range(1, NZ):
            value = value + z_buf[it, d]
        summed[it, chunk(xy)] = value
        rows = summed.at[it, chunk(xy)]
        for d in range(1, NX * NY):
            remote(rows, rows, out_s.at[it, d], out_r.at[it, d], at_xy(d)).start()

    def new_probe_from(it):
        rows = summed.at[it, chunk(xy)]
        for d in range(1, NX * NY):
            arriving = summed.at[it, chunk((xy + NX * NY - d) % (NX * NY))]
            remote(rows, arriving, out_s.at[it, d], out_r.at[it, d], at_xy(d)).wait()
        under = summed[it, 256:384] + 0.2 * PATTERNS
        prb[0] = prb[0] - summed[it, 0:128] / under
        prb[1] = prb[1] - summed[it, 128:256] / under

    loads[0].wait()
    loads[1].wait()
    pl.semaphore_wait(barrier, len(peers))
    copies = halo_copies(0)
    halo_send(0, copies, 1)
    halo_send(0, copies, 2)

    def clear(b, carry):
        for part in range(2):
            zb[b, part, 0:CENTRE] = jnp.zeros((CENTRE, WIDTH), F32)
            zb[b, part, CENTRE + WIDTH:] = jnp.zeros((PLACED - CENTRE - WIDTH, WIDTH), F32)
        return carry

    lax.fori_loop(0, BATCH, clear, 0)
    for load in loads[2:]:
        load.wait()
    for m in range(2):
        tab[2 * m], tab[2 * m + 1] = split(tab32[m])
    halo_finish(0, copies)

    for it in range(ITERS):
        terms[...] = jnp.zeros((TERM_ROWS, WIDTH), F32)

        def some(g, carry):
            patterns(it, g * 8, 4)
            return carry

        lax.fori_loop(0, BATCH // 8, some, 0)
        power = prb[0] * prb[0] + prb[1] * prb[1]
        step = 0.5 / (jnp.max(power) + 1e-6)
        summing = xy_scatter(it)
        folds = fold_send(it)
        interior(it)
        z_gather(it, summing)
        if it + 1 == ITERS:
            start(folds, (2, 3))
        if it + 1 < ITERS:
            copies = halo_copies(it + 1)
        else:
            stores = [
                pltpu.make_async_copy(
                    obj.at[:, 1 + j, HALF:HALF + TILE], new_obj.at[:, :, j * 128:(j + 1) * 128], in_sem.at[7 + j]
                )
                for j in range(2)
            ]
        for j in (1, 2):
            fold_finish(folds, step, j)
            if it + 1 < ITERS:
                halo_send(it + 1, copies, j)
            else:
                stores[j - 1].start()
        xy_gather(it)
        new_probe_from(it)
        if it + 1 < ITERS:
            halo_finish(it + 1, copies)
    stores.append(pltpu.make_async_copy(prb, new_probe, in_sem.at[9]))
    stores[2].start()
    for store in stores:
        store.wait()


def local(object_field, probe_field, amplitudes, positions, shifts):
    hbm = pl.BlockSpec(memory_space=pltpu.HBM)
    dma = pltpu.SemaphoreType.DMA
    scratch = [
        pltpu.SMEM(positions.shape, jnp.int32),
        pltpu.SMEM(shifts.shape, jnp.int32),
        pltpu.VMEM((2, 2 * WIDTH, 2 * WIDTH), F32),
        pltpu.VMEM((4, 2 * WIDTH, 2 * WIDTH), BF16),
        pltpu.VMEM((2, BLOCKS, PAD, WIDTH), F32),
        pltpu.VMEM((2, WIDTH, WIDTH), F32),
        pltpu.VMEM((ITERS, BATCH, WIDTH, WIDTH), F32),
        pltpu.VMEM((BATCH, 2, PLACED, WIDTH), F32),
        pltpu.VMEM((2, BLOCKS, PAD, WIDTH), F32),
        pltpu.VMEM((TERM_ROWS, WIDTH), F32),
        pltpu.VMEM((2, PAD, WIDTH), F32),
        pltpu.VMEM((2, 2, 2, HALF, WIDTH), F32),
        pltpu.VMEM((2, TILE, WIDTH), F32),
        pltpu.VMEM((4, HALF, WIDTH), F32),
        pltpu.VMEM((ITERS, 2, TILE, WIDTH), F32),
        pltpu.VMEM((ITERS, 2, PAD, WIDTH), F32),
        pltpu.VMEM((ITERS, NX * NY, CHUNK, WIDTH), F32),
        pltpu.VMEM((ITERS, 2, CHUNK, WIDTH), F32),
        pltpu.VMEM((ITERS, NZ, CHUNK, WIDTH), F32),
        pltpu.VMEM((ITERS, TERM_ROWS, WIDTH), F32),
        dma((10,)),
        dma((ITERS, 10)), dma((ITERS, 10)),
        dma((ITERS, 10)), dma((ITERS, 10)),
        dma((ITERS, NX * NY)), dma((ITERS, NX * NY)),
        dma((ITERS,)), dma((ITERS,)),
        dma((ITERS, NZ)), dma((ITERS, NZ)),
        dma((ITERS, NX * NY)), dma((ITERS, NX * NY)),
    ]
    return pl.pallas_call(
        kernel,
        out_shape=(
            jax.ShapeDtypeStruct((2, TILE, TILE), F32),
            jax.ShapeDtypeStruct((2, WIDTH, WIDTH), F32),
        ),
        in_specs=[hbm] * 6,
        out_specs=(hbm, hbm),
        scratch_shapes=scratch,
        compiler_params=pltpu.CompilerParams(
            collective_id=0, has_side_effects=True, vmem_limit_bytes=60 * 1024 * 1024
        ),
    )(object_field, probe_field, amplitudes, positions, shifts, jnp.asarray(tables()))


def solution(mesh):
    in_specs = (
        P(None, "row", "col"),
        P(),
        P(None, "row", "col", None, None, None),
        P(None, None, "row", "col", None),
        P(None, None, "row", "col", None),
    )
    out_specs = (P(None, "row", "col"), P())
    return jax.shard_map(local, mesh=mesh, in_specs=in_specs, out_specs=out_specs, check_vma=False)
```

```python
import functools
import math

import jax
import jax.numpy as jnp
import numpy as np
from jax import lax
from jax.experimental import pallas as pl
from jax.experimental.pallas import tpu as pltpu
from jax.sharding import PartitionSpec as P

MESH = pl.DeviceIdType.MESH
F32 = jnp.float32
BF16 = jnp.bfloat16

WIDTH = 128
HALF = 64
TILE = 256
PAD = TILE + 2 * HALF
BLOCKS = 4
BATCH = 16
ITERS = 2
N_ROW = 16
N_COL = 16
NX, NY, NZ = 4, 4, 8
PATTERNS = BATCH * N_ROW * N_COL
TERM_ROWS = 3 * WIDTH
CHUNK = TERM_ROWS // (NX * NY)
CENTRE = 256
PLACED = CENTRE + WIDTH + 256


def tables():
    n = np.arange(WIDTH)
    angle = (np.outer(n, n) % WIDTH) * (2.0 * math.pi / WIDTH)
    c, s = np.cos(angle) / math.sqrt(WIDTH), np.sin(angle) / math.sqrt(WIDTH)
    return np.stack([np.block([[c, s], [-s, c]]), np.block([[c, -s], [s, c]])]).astype(np.float32)


def split(x):
    high = x.astype(BF16)
    return high, (x - high.astype(F32)).astype(BF16)


def mm(a, b):
    return jnp.dot(a, b, preferred_element_type=F32)


def left_mul(high, low, x):
    xh, xl = split(x)
    return mm(high, xh) + mm(high, xl) + mm(low, xh)


def right_mul(x, high, low):
    xh, xl = split(x)
    return mm(xh, high) + mm(xl, high) + mm(xh, low)


def swap_quadrants(y):
    top = jnp.concatenate([y[:WIDTH, :WIDTH], y[WIDTH:, :WIDTH]], axis=1)
    low = jnp.concatenate([y[:WIDTH, WIDTH:], y[WIDTH:, WIDTH:]], axis=1)
    return jnp.concatenate([top, low], axis=0)


def kernel(
    obj_in, probe_in, amp_in, pos_in, shf_in, tab_in, new_obj, new_probe,
    pos, shf, tab32, tab, obj, prb, amp, zb, grad, terms, pack, fold_row, fold_col, fold_cor,
    hpack, hbuf, xy_buf, pair_buf, z_buf, summed,
    in_sem, halo_s, halo_r, fold_s, fold_r, xy_s, xy_r, pair_s, pair_r, z_s, z_r, out_s, out_r,
):
    r, c = lax.axis_index("row"), lax.axis_index("col")
    y, zh, core = r // 4, (r // 2) % 2, r % 2
    zl, x = c // 4, c % 4
    z = zh * 4 + zl
    xy = y * NX + x

    def near(dr, dc):
        return ((r + dr + N_ROW) % N_ROW, (c + dc + N_COL) % N_COL)

    def at_z(d):
        other = (z + d) % NZ
        return (y * 4 + (other // 4) * 2 + core, (other % 4) * 4 + x)

    def at_xy(d):
        other = (xy + d) % (NX * NY)
        return ((other // NX) * 4 + zh * 2 + core, zl * 4 + other % NX)

    partner = (r + 1 - 2 * core, c)
    around = [(-1, 0), (1, 0), (0, -1), (0, 1), (-1, -1), (-1, 1), (1, -1), (1, 1), (-1, 0), (1, 0)]
    around += [(0, -1), (0, 1), (0, -1), (0, 1)]

    barrier = pltpu.get_barrier_semaphore()
    peers = [near(*d) for d in around[:8]]
    peers += [partner] + [at_z(d) for d in range(1, NZ)] + [at_xy(d) for d in range(1, NX * NY)]
    for peer in peers:
        pl.semaphore_signal(barrier, inc=1, device_id=peer, device_id_type=MESH)

    loads = [
        pltpu.make_async_copy(obj_in.at[:, :, 0:128], obj.at[:, 1, HALF:HALF + TILE], in_sem.at[0]),
        pltpu.make_async_copy(obj_in.at[:, :, 128:256], obj.at[:, 2, HALF:HALF + TILE], in_sem.at[1]),
        pltpu.make_async_copy(probe_in, prb, in_sem.at[2]),
        pltpu.make_async_copy(pos_in, pos, in_sem.at[3]),
        pltpu.make_async_copy(shf_in, shf, in_sem.at[4]),
        pltpu.make_async_copy(tab_in, tab32, in_sem.at[5]),
        pltpu.make_async_copy(amp_in.at[:, 0, 0], amp, in_sem.at[6]),
    ]
    for load in loads:
        load.start()

    lane = lax.broadcasted_iota(jnp.int32, (HALF, WIDTH), 1)
    lane_full = lax.broadcasted_iota(jnp.int32, (WIDTH, WIDTH), 1)
    low_half = lane < HALF

    def remote(src, dst, ss, rs, to):
        return pltpu.make_async_remote_copy(
            src_ref=src, dst_ref=dst, send_sem=ss, recv_sem=rs, device_id=to, device_id_type=MESH
        )

    def inside(dr, dc):
        has = [r > 0] if dr < 0 else [r < N_ROW - 1] if dr > 0 else []
        has += [c > 0] if dc < 0 else [c < N_COL - 1] if dc > 0 else []
        return has[0] if len(has) == 1 else jnp.logical_and(*has)

    def start(copies, which):
        for i in which:

            @pl.when(inside(*around[i]))
            def _(copy=copies[i]):
                copy.start()

    def finish(copies, which):
        for i in which:
            dr, dc = around[i]

            @pl.when(inside(dr, dc))
            def _(copy=copies[i]):
                copy.wait_send()

            @pl.when(inside(-dr, -dc))
            def _(copy=copies[i]):
                copy.wait_recv()

    def halo_copies(h):
        src = [
            obj.at[:, 1, 64:128], obj.at[:, 1, 256:320], hpack.at[h, 0], hpack.at[h, 1],
            hpack.at[h, 0, 0:64], hpack.at[h, 1, 0:64], hpack.at[h, 0, 192:256], hpack.at[h, 1, 192:256],
            obj.at[:, 2, 64:128], obj.at[:, 2, 256:320],
        ]
        dst = [
            obj.at[:, 1, 320:384], obj.at[:, 1, 0:64], hbuf.at[h, 0, 64:320], hbuf.at[h, 1, 64:320],
            hbuf.at[h, 0, 320:384], hbuf.at[h, 1, 320:384], hbuf.at[h, 0, 0:64], hbuf.at[h, 1, 0:64],
            obj.at[:, 2, 320:384], obj.at[:, 2, 0:64],
        ]
        return [
            remote(src[i], dst[i], halo_s.at[h, i], halo_r.at[h, i], near(*around[i])) for i in range(10)
        ]

    def halo_pack(h, j, t):
        rows = slice(HALF + 64 * t, HALF + 64 * t + 64)
        to = slice(64 * t, 64 * t + 64)
        re, im = obj[0, j, rows], obj[1, j, rows]
        if j == 1:
            hpack[h, 0, to] = jnp.where(low_half, re, pltpu.roll(im, 64, 1))
        else:
            hpack[h, 1, to] = jnp.where(low_half, pltpu.roll(re, 64, 1), im)

    def halo_edges(h, copies, j):
        for t in (0, 3):
            halo_pack(h, j, t)
        start(copies, (4, 6, 0, 1) if j == 1 else (5, 7, 8, 9))

    def halo_sides(h, copies, j):
        for t in (1, 2):
            halo_pack(h, j, t)
        start(copies, (2,) if j == 1 else (3,))

    def halo_finish(h, copies):
        finish(copies, range(10))
        for t in range(6):
            rows = slice(64 * t, 64 * t + 64)
            dr = -1 if t == 0 else 1 if t == 5 else 0
            right = jnp.where(inside(dr, 1), hbuf[h, 0, rows], 0.0)
            left = jnp.where(inside(dr, -1), hbuf[h, 1, rows], 0.0)
            obj[0, 3, rows] = right
            obj[1, 3, rows] = pltpu.roll(right, 64, 1)
            obj[0, 0, rows] = pltpu.roll(left, 64, 1)
            obj[1, 0, rows] = left

        @pl.when(r == 0)
        def _():
            obj[:, 1:3, 0:64] = jnp.zeros((2, 2, 64, WIDTH), F32)

        @pl.when(r == N_ROW - 1)
        def _():
            obj[:, 1:3, 320:384] = jnp.zeros((2, 2, 64, WIDTH), F32)

    def place_of(it, b):
        u = lax.bitwise_and(pos[0, it, 0, 0, b] + shf[0, it, 0, 0, b], TILE - 1)
        w = lax.bitwise_and(pos[1, it, 0, 0, b] + shf[1, it, 0, 0, b], TILE - 1) + HALF
        return u, lax.shift_right_arithmetic(w, 7), lax.bitwise_and(w, 127)

    def patterns(it, first, count):
        pr, pi = prb[0], prb[1]
        ah, al, bh, bl = tab[0], tab[1], tab[2], tab[3]
        patches, shifts_of, stage = [], [], []
        weight = terms[256:384]
        for p in range(count):
            fields = []
            for i in range(2):
                u, k, s = place_of(it, first + 2 * p + i)
                window = lane_full >= s
                parts = []
                for part in range(2):
                    near_block = obj[part, k, pl.ds(u, WIDTH), :]
                    next_block = obj[part, k + 1, pl.ds(u, WIDTH), :]
                    back_by = lax.bitwise_and(WIDTH - s, 127)
                    parts.append(pltpu.roll(jnp.where(window, near_block, next_block), back_by, 1))
                o_re, o_im = parts
                weight = weight + (o_re * o_re + o_im * o_im)
                patches.append((o_re, o_im))
                shifts_of.append(s)
                fields.append((pr * o_re - pi * o_im, pr * o_im + pi * o_re))
            stage.append(
                jnp.concatenate(
                    [
                        jnp.concatenate([fields[0][0], fields[1][0]], axis=1),
                        jnp.concatenate([fields[0][1], fields[1][1]], axis=1),
                    ],
                    axis=0,
                )
            )
        terms[256:384] = weight
        stage = [left_mul(ah, al, v) for v in stage]
        stage = [right_mul(swap_quadrants(v), bh, bl) for v in stage]
        kept = []
        for p, v in enumerate(stage):
            f_re, f_im = v[:, :WIDTH], v[:, WIDTH:]
            measured = amp[it, pl.ds(first + 2 * p, 2)].reshape(2 * WIDTH, WIDTH)
            keep = 1.0 - measured * lax.rsqrt(jnp.maximum(f_re * f_re + f_im * f_im, 1.0))
            kept.append(jnp.concatenate([keep * f_re, keep * f_im], axis=1))
        stage = [right_mul(v, ah, al) for v in kept]
        stage = [left_mul(bh, bl, swap_quadrants(v)) for v in stage]
        q_re, q_im = terms[0:128], terms[128:256]
        for p, v in enumerate(stage):
            for i in range(2):
                b_re = v[:WIDTH, i * WIDTH:(i + 1) * WIDTH]
                b_im = v[WIDTH:, i * WIDTH:(i + 1) * WIDTH]
                o_re, o_im = patches[2 * p + i]
                q_re = q_re + (o_re * b_re + o_im * b_im)
                q_im = q_im + (o_re * b_im - o_im * b_re)
                s = shifts_of[2 * p + i]
                b = first + 2 * p + i
                zb[b, 0, CENTRE:CENTRE + WIDTH] = pltpu.roll(pr * b_re + pi * b_im, s, 1)
                zb[b, 1, CENTRE:CENTRE + WIDTH] = pltpu.roll(pr * b_im - pi * b_re, s, 1)
        terms[0:128] = q_re
        terms[128:256] = q_im

    def gather_gradient(it, t):
        rows = slice(64 * t, 64 * t + 64) if isinstance(t, int) else pl.ds(pl.multiple_of(64 * t, 64), 64)
        for part in range(2):

            def add(b, acc, part=part):
                u, k, s = place_of(it, b)
                placed = zb[b, part, pl.ds(CENTRE - u + 64 * t, 64), :]
                out = []
                for j in range(BLOCKS):
                    low = jnp.where(k == j, s, WIDTH)
                    high = jnp.where(k + 1 == j, s, 0)
                    mine = jnp.logical_or(lane >= low, lane < high)
                    out.append(acc[j] + jnp.where(mine, placed, 0.0))
                return tuple(out)

            zero = jnp.zeros((64, WIDTH), F32)
            sums = lax.fori_loop(0, BATCH, add, (zero,) * BLOCKS, unroll=8)
            for j in range(BLOCKS):
                grad[part, j, rows] = sums[j]
        pack[0, rows] = jnp.where(low_half, pltpu.roll(grad[0, 0, rows], 64, 1), grad[1, 0, rows])
        pack[1, rows] = jnp.where(low_half, grad[0, 3, rows], pltpu.roll(grad[1, 3, rows], 64, 1))

    def fold_copies(it):
        src = [
            grad.at[:, 1, 0:64], grad.at[:, 1, 320:384], pack.at[0, 128:256], pack.at[1, 128:256],
            pack.at[0, 0:64], pack.at[1, 0:64], pack.at[0, 320:384], pack.at[1, 320:384],
            grad.at[:, 2, 0:64], grad.at[:, 2, 320:384],
            pack.at[0, 64:128], pack.at[1, 64:128], pack.at[0, 256:320], pack.at[1, 256:320],
        ]
        dst = [
            fold_row.at[0, 0], fold_row.at[1, 0], fold_col.at[0, 64:192], fold_col.at[1, 64:192],
            fold_cor.at[0], fold_cor.at[1], fold_cor.at[2], fold_cor.at[3],
            fold_row.at[0, 1], fold_row.at[1, 1],
            fold_col.at[0, 0:64], fold_col.at[1, 0:64], fold_col.at[0, 192:256], fold_col.at[1, 192:256],
        ]
        return [
            remote(src[i], dst[i], fold_s.at[it, i], fold_r.at[it, i], near(*around[i])) for i in range(14)
        ]

    def fold_send(it):
        copies = fold_copies(it)
        gather_gradient(it, 0)
        start(copies, (4, 5, 0, 8))
        gather_gradient(it, 5)
        start(copies, (6, 7, 1, 9))
        gather_gradient(it, 1)
        gather_gradient(it, 4)
        if it + 1 < ITERS:
            start(copies, (10, 11, 12, 13))

        def middle(t, carry):
            gather_gradient(it, t)
            return carry

        lax.fori_loop(2, 4, middle, 0)
        if it + 1 < ITERS:
            start(copies, (2, 3))
        return copies

    def fold_finish(copies, step, j, edges):
        if edges:
            finish(copies, (0, 1, 5, 7, 11, 13) if j == 1 else (8, 9, 4, 6, 10, 12))
        else:
            finish(copies, (3,) if j == 1 else (2,))
        up, down = inside(-1, 0), inside(1, 0)
        beside = inside(0, -1 if j == 1 else 1)
        for t in (0, 3) if edges else (1, 2):
            rows = slice(HALF + 64 * t, HALF + 64 * t + 64)
            at = slice(64 * t, 64 * t + 64)
            side = jnp.where(beside, fold_col[2 - j, at], 0.0)
            if t == 0:
                side = side + jnp.where(jnp.logical_and(up, beside), fold_cor[3 if j == 1 else 2], 0.0)
            if t == 3:
                side = side + jnp.where(jnp.logical_and(down, beside), fold_cor[1 if j == 1 else 0], 0.0)
            if j == 1:
                added = [jnp.where(low_half, side, 0.0), jnp.where(low_half, pltpu.roll(side, 64, 1), 0.0)]
            else:
                added = [jnp.where(low_half, 0.0, pltpu.roll(side, 64, 1)), jnp.where(low_half, 0.0, side)]
            for part in range(2):
                g = grad[part, j, rows] + added[part]
                if t == 0:
                    g = g + jnp.where(up, fold_row[1, j - 1, part], 0.0)
                if t == 3:
                    g = g + jnp.where(down, fold_row[0, j - 1, part], 0.0)
                obj[part, j, rows] = obj[part, j, rows] - step * g

    def chunk(i):
        return pl.ds(pl.multiple_of(i * CHUNK, 8), CHUNK)

    def xy_scatter(it):
        copies = []
        for d in range(1, NX * NY):
            copies.append(
                remote(
                    terms.at[chunk((xy + d) % (NX * NY))], xy_buf.at[it, d],
                    xy_s.at[it, d], xy_r.at[it, d], at_xy(d),
                )
            )
            copies[-1].start()
        return copies

    def z_gather(it, before):
        for copy in before:
            copy.wait()
        value = terms[chunk(xy)]
        for d in range(1, NX * NY):
            value = value + xy_buf[it, d]
        pair_buf[it, 0] = value
        swap = remote(pair_buf.at[it, 0], pair_buf.at[it, 1], pair_s.at[it], pair_r.at[it], partner)
        swap.start()
        swap.wait()
        z_buf[it, z] = value + pair_buf[it, 1]
        for d in range(1, NZ):
            remote(z_buf.at[it, z], z_buf.at[it, z], z_s.at[it, d], z_r.at[it, d], at_z(d)).start()

    def xy_gather(it):
        for d in range(1, NZ):
            arriving = z_buf.at[it, (z + NZ - d) % NZ]
            remote(z_buf.at[it, z], arriving, z_s.at[it, d], z_r.at[it, d], at_z(d)).wait()
        value = z_buf[it, 0]
        for d in range(1, NZ):
            value = value + z_buf[it, d]
        summed[it, chunk(xy)] = value
        rows = summed.at[it, chunk(xy)]
        for d in range(1, NX * NY):
            remote(rows, rows, out_s.at[it, d], out_r.at[it, d], at_xy(d)).start()

    def new_probe_from(it):
        rows = summed.at[it, chunk(xy)]
        for d in range(1, NX * NY):
            arriving = summed.at[it, chunk((xy + NX * NY - d) % (NX * NY))]
            remote(rows, arriving, out_s.at[it, d], out_r.at[it, d], at_xy(d)).wait()
        under = summed[it, 256:384] + 0.2 * PATTERNS
        for part in range(2):
            prb[part] = prb[part] - summed[it, part * 128:(part + 1) * 128] / under

    loads[0].wait()
    loads[1].wait()
    pl.semaphore_wait(barrier, len(peers))
    copies = halo_copies(0)
    for j in (1, 2):
        halo_edges(0, copies, j)
    for j in (1, 2):
        halo_sides(0, copies, j)

    def clear(b, carry):
        for part in range(2):
            zb[b, part, 0:CENTRE] = jnp.zeros((CENTRE, WIDTH), F32)
            zb[b, part, CENTRE + WIDTH:] = jnp.zeros((PLACED - CENTRE - WIDTH, WIDTH), F32)
        return carry

    lax.fori_loop(0, BATCH, clear, 0)
    for load in loads[2:]:
        load.wait()
    for m in range(2):
        tab[2 * m], tab[2 * m + 1] = split(tab32[m])
    halo_finish(0, copies)

    for it in range(ITERS):
        terms[...] = jnp.zeros((TERM_ROWS, WIDTH), F32)

        patterns(it, 0, BATCH // 2)
        summing = xy_scatter(it)
        folds = fold_send(it)
        power = prb[0] * prb[0] + prb[1] * prb[1]
        step = 0.5 / (jnp.max(power) + 1e-6)
        z_gather(it, summing)
        if it + 1 == ITERS:
            start(folds, (2, 3, 10, 11, 12, 13))
        if it + 1 < ITERS:
            copies = halo_copies(it + 1)
        else:
            stores = [
                pltpu.make_async_copy(
                    obj.at[:, 1 + j, HALF:HALF + TILE], new_obj.at[:, :, j * 128:(j + 1) * 128], in_sem.at[7 + j]
                )
                for j in range(2)
            ]
        for edges in (True, False):
            for j in (1, 2):
                fold_finish(folds, step, j, edges)
                if it + 1 == ITERS:
                    if not edges:
                        stores[j - 1].start()
                elif edges:
                    halo_edges(it + 1, copies, j)
                else:
                    halo_sides(it + 1, copies, j)
        xy_gather(it)
        new_probe_from(it)
        if it + 1 < ITERS:
            halo_finish(it + 1, copies)
    stores.append(pltpu.make_async_copy(prb, new_probe, in_sem.at[9]))
    stores[2].start()
    for store in stores:
        store.wait()


def local(object_field, probe_field, amplitudes, positions, shifts):
    hbm = pl.BlockSpec(memory_space=pltpu.HBM)
    dma = pltpu.SemaphoreType.DMA
    scratch = [
        pltpu.SMEM(positions.shape, jnp.int32),
        pltpu.SMEM(shifts.shape, jnp.int32),
        pltpu.VMEM((2, 2 * WIDTH, 2 * WIDTH), F32),
        pltpu.VMEM((4, 2 * WIDTH, 2 * WIDTH), BF16),
        pltpu.VMEM((2, BLOCKS, PAD, WIDTH), F32),
        pltpu.VMEM((2, WIDTH, WIDTH), F32),
        pltpu.VMEM((ITERS, BATCH, WIDTH, WIDTH), F32),
        pltpu.VMEM((BATCH, 2, PLACED, WIDTH), F32),
        pltpu.VMEM((2, BLOCKS, PAD, WIDTH), F32),
        pltpu.VMEM((TERM_ROWS, WIDTH), F32),
        pltpu.VMEM((2, PAD, WIDTH), F32),
        pltpu.VMEM((2, 2, 2, HALF, WIDTH), F32),
        pltpu.VMEM((2, TILE, WIDTH), F32),
        pltpu.VMEM((4, HALF, WIDTH), F32),
        pltpu.VMEM((ITERS, 2, TILE, WIDTH), F32),
        pltpu.VMEM((ITERS, 2, PAD, WIDTH), F32),
        pltpu.VMEM((ITERS, NX * NY, CHUNK, WIDTH), F32),
        pltpu.VMEM((ITERS, 2, CHUNK, WIDTH), F32),
        pltpu.VMEM((ITERS, NZ, CHUNK, WIDTH), F32),
        pltpu.VMEM((ITERS, TERM_ROWS, WIDTH), F32),
        dma((10,)),
        dma((ITERS, 10)), dma((ITERS, 10)),
        dma((ITERS, 14)), dma((ITERS, 14)),
        dma((ITERS, NX * NY)), dma((ITERS, NX * NY)),
        dma((ITERS,)), dma((ITERS,)),
        dma((ITERS, NZ)), dma((ITERS, NZ)),
        dma((ITERS, NX * NY)), dma((ITERS, NX * NY)),
    ]
    return pl.pallas_call(
        kernel,
        out_shape=(
            jax.ShapeDtypeStruct((2, TILE, TILE), F32),
            jax.ShapeDtypeStruct((2, WIDTH, WIDTH), F32),
        ),
        in_specs=[hbm] * 6,
        out_specs=(hbm, hbm),
        scratch_shapes=scratch,
        compiler_params=pltpu.CompilerParams(
            collective_id=0, has_side_effects=True, vmem_limit_bytes=60 * 1024 * 1024
        ),
    )(object_field, probe_field, amplitudes, positions, shifts, jnp.asarray(tables()))


def solution(mesh):
    in_specs = (
        P(None, "row", "col"),
        P(),
        P(None, "row", "col", None, None, None),
        P(None, None, "row", "col", None),
        P(None, None, "row", "col", None),
    )
    out_specs = (P(None, "row", "col"), P())
    return jax.shard_map(local, mesh=mesh, in_specs=in_specs, out_specs=out_specs, check_vma=False)
```

```python
import functools
import math

import jax
import jax.numpy as jnp
import numpy as np
from jax import lax
from jax.experimental import pallas as pl
from jax.experimental.pallas import tpu as pltpu
from jax.sharding import PartitionSpec as P

MESH = pl.DeviceIdType.MESH
F32 = jnp.float32
BF16 = jnp.bfloat16

WIDTH = 128
HALF = 64
TILE = 256
PAD = TILE + 2 * HALF
BLOCKS = 4
BATCH = 16
ITERS = 2
N_ROW = 16
N_COL = 16
NX, NY, NZ = 4, 4, 8
PATTERNS = BATCH * N_ROW * N_COL
TERM_ROWS = 3 * WIDTH
CHUNK = TERM_ROWS // (NX * NY)
CENTRE = 256
PLACED = CENTRE + WIDTH + 256


def tables():
    n = np.arange(WIDTH)
    angle = (np.outer(n, n) % WIDTH) * (2.0 * math.pi / WIDTH)
    c, s = np.cos(angle) / math.sqrt(WIDTH), np.sin(angle) / math.sqrt(WIDTH)
    return np.stack([np.block([[c, s], [-s, c]]), np.block([[c, -s], [s, c]])]).astype(np.float32)


def split(x):
    high = x.astype(BF16)
    return high, (x - high.astype(F32)).astype(BF16)


def mm(a, b):
    return jnp.dot(a, b, preferred_element_type=F32)


def left_mul(high, low, x):
    xh, xl = split(x)
    return mm(high, xh) + mm(high, xl) + mm(low, xh)


def right_mul(x, high, low):
    xh, xl = split(x)
    return mm(xh, high) + mm(xl, high) + mm(xh, low)


def swap_quadrants(y):
    top = jnp.concatenate([y[:WIDTH, :WIDTH], y[WIDTH:, :WIDTH]], axis=1)
    low = jnp.concatenate([y[:WIDTH, WIDTH:], y[WIDTH:, WIDTH:]], axis=1)
    return jnp.concatenate([top, low], axis=0)


def kernel(
    obj_in, probe_in, amp_in, pos_in, shf_in, tab_in, new_obj, new_probe,
    pos, shf, tab32, tab, obj, prb, amp, zb, grad, terms, pack, fold_row, fold_col, fold_cor,
    hpack, hbuf, xy_buf, pair_buf, z_buf, summed,
    in_sem, halo_s, halo_r, fold_s, fold_r, xy_s, xy_r, pair_s, pair_r, z_s, z_r, out_s, out_r,
):
    r, c = lax.axis_index("row"), lax.axis_index("col")
    y, zh, core = r // 4, (r // 2) % 2, r % 2
    zl, x = c // 4, c % 4
    z = zh * 4 + zl
    xy = y * NX + x

    def near(dr, dc):
        return ((r + dr + N_ROW) % N_ROW, (c + dc + N_COL) % N_COL)

    def at_z(d):
        other = (z + d) % NZ
        return (y * 4 + (other // 4) * 2 + core, (other % 4) * 4 + x)

    def at_xy(d):
        other = (xy + d) % (NX * NY)
        return ((other // NX) * 4 + zh * 2 + core, zl * 4 + other % NX)

    partner = (r + 1 - 2 * core, c)
    around = [(-1, 0), (1, 0), (0, -1), (0, 1), (-1, -1), (-1, 1), (1, -1), (1, 1), (-1, 0), (1, 0)]
    around += [(0, -1), (0, 1), (0, -1), (0, 1)]

    barrier = pltpu.get_barrier_semaphore()
    peers = [near(*d) for d in around[:8]]
    peers += [partner] + [at_z(d) for d in range(1, NZ)] + [at_xy(d) for d in range(1, NX * NY)]
    for peer in peers:
        pl.semaphore_signal(barrier, inc=1, device_id=peer, device_id_type=MESH)

    loads = [
        pltpu.make_async_copy(obj_in.at[:, :, 0:128], obj.at[:, 1, HALF:HALF + TILE], in_sem.at[0]),
        pltpu.make_async_copy(obj_in.at[:, :, 128:256], obj.at[:, 2, HALF:HALF + TILE], in_sem.at[1]),
        pltpu.make_async_copy(probe_in, prb, in_sem.at[2]),
        pltpu.make_async_copy(pos_in, pos, in_sem.at[3]),
        pltpu.make_async_copy(shf_in, shf, in_sem.at[4]),
        pltpu.make_async_copy(tab_in, tab32, in_sem.at[5]),
        pltpu.make_async_copy(amp_in.at[:, 0, 0], amp, in_sem.at[6]),
    ]
    for load in loads:
        load.start()

    lane = lax.broadcasted_iota(jnp.int32, (HALF, WIDTH), 1)
    lane_full = lax.broadcasted_iota(jnp.int32, (WIDTH, WIDTH), 1)
    low_half = lane < HALF

    def remote(src, dst, ss, rs, to):
        return pltpu.make_async_remote_copy(
            src_ref=src, dst_ref=dst, send_sem=ss, recv_sem=rs, device_id=to, device_id_type=MESH
        )

    def inside(dr, dc):
        has = [r > 0] if dr < 0 else [r < N_ROW - 1] if dr > 0 else []
        has += [c > 0] if dc < 0 else [c < N_COL - 1] if dc > 0 else []
        return has[0] if len(has) == 1 else jnp.logical_and(*has)

    def start(copies, which):
        for i in which:

            @pl.when(inside(*around[i]))
            def _(copy=copies[i]):
                copy.start()

    def finish(copies, which):
        for i in which:
            dr, dc = around[i]

            @pl.when(inside(dr, dc))
            def _(copy=copies[i]):
                copy.wait_send()

            @pl.when(inside(-dr, -dc))
            def _(copy=copies[i]):
                copy.wait_recv()

    def halo_copies(h):
        src = [
            obj.at[:, 1, 64:128], obj.at[:, 1, 256:320], hpack.at[h, 0], hpack.at[h, 1],
            hpack.at[h, 0, 0:64], hpack.at[h, 1, 0:64], hpack.at[h, 0, 192:256], hpack.at[h, 1, 192:256],
            obj.at[:, 2, 64:128], obj.at[:, 2, 256:320],
        ]
        dst = [
            obj.at[:, 1, 320:384], obj.at[:, 1, 0:64], hbuf.at[h, 0, 64:320], hbuf.at[h, 1, 64:320],
            hbuf.at[h, 0, 320:384], hbuf.at[h, 1, 320:384], hbuf.at[h, 0, 0:64], hbuf.at[h, 1, 0:64],
            obj.at[:, 2, 320:384], obj.at[:, 2, 0:64],
        ]
        return [
            remote(src[i], dst[i], halo_s.at[h, i], halo_r.at[h, i], near(*around[i])) for i in range(10)
        ]

    def halo_pack(h, j, t):
        rows = slice(HALF + 64 * t, HALF + 64 * t + 64)
        to = slice(64 * t, 64 * t + 64)
        re, im = obj[0, j, rows], obj[1, j, rows]
        if j == 1:
            hpack[h, 0, to] = jnp.where(low_half, re, pltpu.roll(im, 64, 1))
        else:
            hpack[h, 1, to] = jnp.where(low_half, pltpu.roll(re, 64, 1), im)

    def halo_edges(h, copies, j):
        for t in (0, 3):
            halo_pack(h, j, t)
        start(copies, (4, 6, 0, 1) if j == 1 else (5, 7, 8, 9))

    def halo_sides(h, copies, j):
        for t in (1, 2):
            halo_pack(h, j, t)
        start(copies, (2,) if j == 1 else (3,))

    def halo_finish(h, copies):
        finish(copies, range(10))
        for t in range(6):
            rows = slice(64 * t, 64 * t + 64)
            dr = -1 if t == 0 else 1 if t == 5 else 0
            right = jnp.where(inside(dr, 1), hbuf[h, 0, rows], 0.0)
            left = jnp.where(inside(dr, -1), hbuf[h, 1, rows], 0.0)
            obj[0, 3, rows] = right
            obj[1, 3, rows] = pltpu.roll(right, 64, 1)
            obj[0, 0, rows] = pltpu.roll(left, 64, 1)
            obj[1, 0, rows] = left

        @pl.when(r == 0)
        def _():
            obj[:, 1:3, 0:64] = jnp.zeros((2, 2, 64, WIDTH), F32)

        @pl.when(r == N_ROW - 1)
        def _():
            obj[:, 1:3, 320:384] = jnp.zeros((2, 2, 64, WIDTH), F32)

    def place_of(it, b):
        u = lax.bitwise_and(pos[0, it, 0, 0, b] + shf[0, it, 0, 0, b], TILE - 1)
        w = lax.bitwise_and(pos[1, it, 0, 0, b] + shf[1, it, 0, 0, b], TILE - 1) + HALF
        return u, lax.shift_right_arithmetic(w, 7), lax.bitwise_and(w, 127)

    def patterns(it, first, count):
        pr, pi = prb[0], prb[1]
        ah, al, bh, bl = tab[0], tab[1], tab[2], tab[3]
        patches, shifts_of, stage = [], [], []
        weight = terms[256:384]
        for p in range(count):
            fields = []
            for i in range(2):
                u, k, s = place_of(it, first + 2 * p + i)
                window = lane_full >= s
                parts = []
                for part in range(2):
                    near_block = obj[part, k, pl.ds(u, WIDTH), :]
                    next_block = obj[part, k + 1, pl.ds(u, WIDTH), :]
                    back_by = lax.bitwise_and(WIDTH - s, 127)
                    parts.append(pltpu.roll(jnp.where(window, near_block, next_block), back_by, 1))
                o_re, o_im = parts
                weight = weight + (o_re * o_re + o_im * o_im)
                patches.append((o_re, o_im))
                shifts_of.append(s)
                fields.append((pr * o_re - pi * o_im, pr * o_im + pi * o_re))
            stage.append(
                jnp.concatenate(
                    [
                        jnp.concatenate([fields[0][0], fields[1][0]], axis=1),
                        jnp.concatenate([fields[0][1], fields[1][1]], axis=1),
                    ],
                    axis=0,
                )
            )
        terms[256:384] = weight
        stage = [left_mul(ah, al, v) for v in stage]
        stage = [right_mul(swap_quadrants(v), bh, bl) for v in stage]
        kept = []
        for p, v in enumerate(stage):
            f_re, f_im = v[:, :WIDTH], v[:, WIDTH:]
            measured = amp[it, pl.ds(first + 2 * p, 2)].reshape(2 * WIDTH, WIDTH)
            keep = 1.0 - measured * lax.rsqrt(jnp.maximum(f_re * f_re + f_im * f_im, 1.0))
            kept.append(jnp.concatenate([keep * f_re, keep * f_im], axis=1))
        stage = [right_mul(v, ah, al) for v in kept]
        stage = [left_mul(bh, bl, swap_quadrants(v)) for v in stage]
        q_re, q_im = terms[0:128], terms[128:256]
        for p, v in enumerate(stage):
            for i in range(2):
                b_re = v[:WIDTH, i * WIDTH:(i + 1) * WIDTH]
                b_im = v[WIDTH:, i * WIDTH:(i + 1) * WIDTH]
                o_re, o_im = patches[2 * p + i]
                q_re = q_re + (o_re * b_re + o_im * b_im)
                q_im = q_im + (o_re * b_im - o_im * b_re)
                s = shifts_of[2 * p + i]
                b = first + 2 * p + i
                zb[b, 0, CENTRE:CENTRE + WIDTH] = pltpu.roll(pr * b_re + pi * b_im, s, 1)
                zb[b, 1, CENTRE:CENTRE + WIDTH] = pltpu.roll(pr * b_im - pi * b_re, s, 1)
        terms[0:128] = q_re
        terms[128:256] = q_im

    def gather_gradient(it, t):
        rows = slice(64 * t, 64 * t + 64) if isinstance(t, int) else pl.ds(pl.multiple_of(64 * t, 64), 64)
        for part in range(2):

            def add(b, acc, part=part):
                u, k, s = place_of(it, b)
                placed = zb[b, part, pl.ds(CENTRE - u + 64 * t, 64), :]
                out = []
                for j in range(BLOCKS):
                    low = jnp.where(k == j, s, WIDTH)
                    high = jnp.where(k + 1 == j, s, 0)
                    mine = jnp.logical_or(lane >= low, lane < high)
                    out.append(acc[j] + jnp.where(mine, placed, 0.0))
                return tuple(out)

            zero = jnp.zeros((64, WIDTH), F32)
            sums = lax.fori_loop(0, BATCH, add, (zero,) * BLOCKS, unroll=8)
            for j in range(BLOCKS):
                grad[part, j, rows] = sums[j]
        pack[0, rows] = jnp.where(low_half, pltpu.roll(grad[0, 0, rows], 64, 1), grad[1, 0, rows])
        pack[1, rows] = jnp.where(low_half, grad[0, 3, rows], pltpu.roll(grad[1, 3, rows], 64, 1))

    def fold_copies(it):
        src = [
            grad.at[:, 1, 0:64], grad.at[:, 1, 320:384], pack.at[0, 128:256], pack.at[1, 128:256],
            pack.at[0, 0:64], pack.at[1, 0:64], pack.at[0, 320:384], pack.at[1, 320:384],
            grad.at[:, 2, 0:64], grad.at[:, 2, 320:384],
            pack.at[0, 64:128], pack.at[1, 64:128], pack.at[0, 256:320], pack.at[1, 256:320],
        ]
        dst = [
            fold_row.at[0, 0], fold_row.at[1, 0], fold_col.at[0, 64:192], fold_col.at[1, 64:192],
            fold_cor.at[0], fold_cor.at[1], fold_cor.at[2], fold_cor.at[3],
            fold_row.at[0, 1], fold_row.at[1, 1],
            fold_col.at[0, 0:64], fold_col.at[1, 0:64], fold_col.at[0, 192:256], fold_col.at[1, 192:256],
        ]
        return [
            remote(src[i], dst[i], fold_s.at[it, i], fold_r.at[it, i], near(*around[i])) for i in range(14)
        ]

    def fold_send(it):
        copies = fold_copies(it)
        gather_gradient(it, 0)
        start(copies, (4, 5, 0, 8))
        gather_gradient(it, 5)
        start(copies, (6, 7, 1, 9))
        gather_gradient(it, 1)
        gather_gradient(it, 4)
        if it + 1 < ITERS:
            start(copies, (10, 11, 12, 13))

        def middle(t, carry):
            gather_gradient(it, t)
            return carry

        lax.fori_loop(2, 4, middle, 0)
        if it + 1 < ITERS:
            start(copies, (2, 3))
        return copies

    def fold_finish(copies, step, j, edges):
        if edges:
            finish(copies, (0, 1, 5, 7, 11, 13) if j == 1 else (8, 9, 4, 6, 10, 12))
        else:
            finish(copies, (3,) if j == 1 else (2,))
        up, down = inside(-1, 0), inside(1, 0)
        beside = inside(0, -1 if j == 1 else 1)
        for t in (0, 3) if edges else (1, 2):
            rows = slice(HALF + 64 * t, HALF + 64 * t + 64)
            at = slice(64 * t, 64 * t + 64)
            side = jnp.where(beside, fold_col[2 - j, at], 0.0)
            if t == 0:
                side = side + jnp.where(jnp.logical_and(up, beside), fold_cor[3 if j == 1 else 2], 0.0)
            if t == 3:
                side = side + jnp.where(jnp.logical_and(down, beside), fold_cor[1 if j == 1 else 0], 0.0)
            if j == 1:
                added = [jnp.where(low_half, side, 0.0), jnp.where(low_half, pltpu.roll(side, 64, 1), 0.0)]
            else:
                added = [jnp.where(low_half, 0.0, pltpu.roll(side, 64, 1)), jnp.where(low_half, 0.0, side)]
            for part in range(2):
                g = grad[part, j, rows] + added[part]
                if t == 0:
                    g = g + jnp.where(up, fold_row[1, j - 1, part], 0.0)
                if t == 3:
                    g = g + jnp.where(down, fold_row[0, j - 1, part], 0.0)
                obj[part, j, rows] = obj[part, j, rows] - step * g

    def chunk(i):
        return pl.ds(pl.multiple_of(i * CHUNK, 8), CHUNK)

    def xy_scatter(it):
        copies = []
        for d in range(1, NX * NY):
            copies.append(
                remote(
                    terms.at[chunk((xy + d) % (NX * NY))], xy_buf.at[it, d],
                    xy_s.at[it, d], xy_r.at[it, d], at_xy(d),
                )
            )
            copies[-1].start()
        return copies

    def z_gather(it, before):
        for copy in before:
            copy.wait()
        value = terms[chunk(xy)]
        for d in range(1, NX * NY):
            value = value + xy_buf[it, d]
        pair_buf[it, 0] = value
        swap = remote(pair_buf.at[it, 0], pair_buf.at[it, 1], pair_s.at[it], pair_r.at[it], partner)
        swap.start()
        swap.wait()
        z_buf[it, z] = value + pair_buf[it, 1]
        for d in range(1, NZ):
            remote(z_buf.at[it, z], z_buf.at[it, z], z_s.at[it, d], z_r.at[it, d], at_z(d)).start()

    def xy_gather(it):
        for d in range(1, NZ):
            arriving = z_buf.at[it, (z + NZ - d) % NZ]
            remote(z_buf.at[it, z], arriving, z_s.at[it, d], z_r.at[it, d], at_z(d)).wait()
        value = z_buf[it, 0]
        for d in range(1, NZ):
            value = value + z_buf[it, d]
        summed[it, chunk(xy)] = value
        rows = summed.at[it, chunk(xy)]
        for d in range(1, NX * NY):
            remote(rows, rows, out_s.at[it, d], out_r.at[it, d], at_xy(d)).start()

    def new_probe_from(it):
        rows = summed.at[it, chunk(xy)]
        for d in range(1, NX * NY):
            arriving = summed.at[it, chunk((xy + NX * NY - d) % (NX * NY))]
            remote(rows, arriving, out_s.at[it, d], out_r.at[it, d], at_xy(d)).wait()
        under = summed[it, 256:384] + 0.2 * PATTERNS
        for part in range(2):
            prb[part] = prb[part] - summed[it, part * 128:(part + 1) * 128] / under

    loads[0].wait()
    loads[1].wait()
    pl.semaphore_wait(barrier, len(peers))
    copies = halo_copies(0)
    for j in (1, 2):
        halo_edges(0, copies, j)
    for j in (1, 2):
        halo_sides(0, copies, j)

    def clear(b, carry):
        for part in range(2):
            zb[b, part, 0:CENTRE] = jnp.zeros((CENTRE, WIDTH), F32)
            zb[b, part, CENTRE + WIDTH:] = jnp.zeros((PLACED - CENTRE - WIDTH, WIDTH), F32)
        return carry

    lax.fori_loop(0, BATCH, clear, 0)
    for load in loads[2:]:
        load.wait()
    for m in range(2):
        tab[2 * m], tab[2 * m + 1] = split(tab32[m])
    halo_finish(0, copies)

    for it in range(ITERS):
        terms[...] = jnp.zeros((TERM_ROWS, WIDTH), F32)

        patterns(it, 0, BATCH // 2)
        summing = xy_scatter(it)
        folds = fold_send(it)
        power = prb[0] * prb[0] + prb[1] * prb[1]
        step = 0.5 / (jnp.max(power) + 1e-6)
        z_gather(it, summing)
        if it + 1 == ITERS:
            start(folds, (2, 3, 10, 11, 12, 13))
        if it + 1 < ITERS:
            copies = halo_copies(it + 1)
        else:
            stores = [
                pltpu.make_async_copy(
                    obj.at[:, 1 + j, HALF:HALF + TILE], new_obj.at[:, :, j * 128:(j + 1) * 128], in_sem.at[7 + j]
                )
                for j in range(2)
            ]
        if it + 1 == ITERS:
            xy_gather(it)
        for edges in (True, False):
            for j in (1, 2):
                fold_finish(folds, step, j, edges)
                if it + 1 == ITERS:
                    if not edges:
                        stores[j - 1].start()
                elif edges:
                    halo_edges(it + 1, copies, j)
                else:
                    halo_sides(it + 1, copies, j)
        if it + 1 < ITERS:
            xy_gather(it)
        new_probe_from(it)
        if it + 1 < ITERS:
            halo_finish(it + 1, copies)
    stores.append(pltpu.make_async_copy(prb, new_probe, in_sem.at[9]))
    stores[2].start()
    for store in stores:
        store.wait()


def local(object_field, probe_field, amplitudes, positions, shifts):
    hbm = pl.BlockSpec(memory_space=pltpu.HBM)
    dma = pltpu.SemaphoreType.DMA
    scratch = [
        pltpu.SMEM(positions.shape, jnp.int32),
        pltpu.SMEM(shifts.shape, jnp.int32),
        pltpu.VMEM((2, 2 * WIDTH, 2 * WIDTH), F32),
        pltpu.VMEM((4, 2 * WIDTH, 2 * WIDTH), BF16),
        pltpu.VMEM((2, BLOCKS, PAD, WIDTH), F32),
        pltpu.VMEM((2, WIDTH, WIDTH), F32),
        pltpu.VMEM((ITERS, BATCH, WIDTH, WIDTH), F32),
        pltpu.VMEM((BATCH, 2, PLACED, WIDTH), F32),
        pltpu.VMEM((2, BLOCKS, PAD, WIDTH), F32),
        pltpu.VMEM((TERM_ROWS, WIDTH), F32),
        pltpu.VMEM((2, PAD, WIDTH), F32),
        pltpu.VMEM((2, 2, 2, HALF, WIDTH), F32),
        pltpu.VMEM((2, TILE, WIDTH), F32),
        pltpu.VMEM((4, HALF, WIDTH), F32),
        pltpu.VMEM((ITERS, 2, TILE, WIDTH), F32),
        pltpu.VMEM((ITERS, 2, PAD, WIDTH), F32),
        pltpu.VMEM((ITERS, NX * NY, CHUNK, WIDTH), F32),
        pltpu.VMEM((ITERS, 2, CHUNK, WIDTH), F32),
        pltpu.VMEM((ITERS, NZ, CHUNK, WIDTH), F32),
        pltpu.VMEM((ITERS, TERM_ROWS, WIDTH), F32),
        dma((10,)),
        dma((ITERS, 10)), dma((ITERS, 10)),
        dma((ITERS, 14)), dma((ITERS, 14)),
        dma((ITERS, NX * NY)), dma((ITERS, NX * NY)),
        dma((ITERS,)), dma((ITERS,)),
        dma((ITERS, NZ)), dma((ITERS, NZ)),
        dma((ITERS, NX * NY)), dma((ITERS, NX * NY)),
    ]
    return pl.pallas_call(
        kernel,
        out_shape=(
            jax.ShapeDtypeStruct((2, TILE, TILE), F32),
            jax.ShapeDtypeStruct((2, WIDTH, WIDTH), F32),
        ),
        in_specs=[hbm] * 6,
        out_specs=(hbm, hbm),
        scratch_shapes=scratch,
        compiler_params=pltpu.CompilerParams(
            collective_id=0, has_side_effects=True, vmem_limit_bytes=60 * 1024 * 1024
        ),
    )(object_field, probe_field, amplitudes, positions, shifts, jnp.asarray(tables()))


def solution(mesh):
    in_specs = (
        P(None, "row", "col"),
        P(),
        P(None, "row", "col", None, None, None),
        P(None, None, "row", "col", None),
        P(None, None, "row", "col", None),
    )
    out_specs = (P(None, "row", "col"), P())
    return jax.shard_map(local, mesh=mesh, in_specs=in_specs, out_specs=out_specs, check_vma=False)
```
